512 devices in a mesh: fsdp: 64 (over z, x), seq: 8 (over y, core).
Axes of the slice: x: 4, y: 4, z: 16, core: 2. Of those that a mesh axis runs over, the one named last changes fastest.
Arguments:
- queries: bfloat16 [65536, 2048], P(('fsdp', 'seq')), may hold values from -20 to 20
- neighbours: bfloat16 [131072, 896], P(('fsdp', 'seq')), may hold values from -6 to 6
- neighbour_slot: int32 [2048], P('fsdp'), may hold values from 0 to 2047, as said below
- enc_gain: float32 [896], replicated, may hold values from 0.1 to 1.9
- enc_up: bfloat16 [896, 1792], P(None, 'fsdp'), may hold values from -0.1875 to 0.1875
- enc_down: bfloat16 [1792, 896], P('fsdp'), may hold values from -0.125 to 0.125
- key_proj: bfloat16 [896, 2048], P(None, 'fsdp'), may hold values from -0.1875 to 0.1875
- value_proj: bfloat16 [896, 2048], P(None, 'fsdp'), may hold values from -0.1875 to 0.1875
- grad_attn: bfloat16 [65536, 2048], P(('fsdp', 'seq')), may hold values from -6 to 6
Outputs:
- attended: bfloat16 [65536, 2048], P(('fsdp', 'seq'))
- grad_queries: bfloat16 [65536, 2048], P(('fsdp', 'seq'))
- grad_encoded: bfloat16 [131072, 896], P(('fsdp', 'seq'))
The draws below stay inside these ranges and needn't reach their ends.
Inputs may be any that keep to these rules, and one draw needn't show every extreme that they name: neighbour_slot is a permutation of the 2048 slots; a neighbour's slot belongs to a span on a device of the same index of fsdp as the neighbour; the 4 neighbours of one device fill exactly 1 slot on each of 4 devices of its seq group and none on the other 4.
All inputs are finite; a program needn't handle non-finite values.
Results may differ from the reference program's by a relative error of at most 0.015.
The reference program's roundings to bfloat16 on the way count: a program that leaves them out, or rounds other values in their place, can miss the bound.
Values may be sent and summed in bfloat16 or wider, within the bound.
No kernel may reach another device: no remote copies, remote signals or barrier semaphores. Data moves between devices by JAX's collectives and lax.ppermute only.
A program may use at most 64 MiB of HBM per device.

```python
import jax
import jax.numpy as jnp
from jax import lax

E = 896
EF = 1792
HEADS = 16
HD = 128
CL = 64
NLEN = 64
NPC = 2
CH_DEV = 2
SPANS = 1024
NBRS = 2048
N_FSDP = 64
N_SEQ = 8


def draw_queries(key, part):
    dimensions = (CH_DEV * N_FSDP * N_SEQ * CL, HEADS * HD)
    drawn = jnp.clip(jax.random.normal(key, dimensions, jnp.float32), -5.0, 5.0)
    return drawn.astype(jnp.bfloat16)


def draw_neighbour_slot(key, part):
    per_device = CH_DEV * NPC
    reach = min(N_SEQ, per_device)
    capacity = per_device // reach
    first_key = jax.random.fold_in(key, 11)
    second_key = jax.random.fold_in(key, 12)
    third_key = jax.random.fold_in(key, 13)
    order = jax.vmap(lambda sub_key: jax.random.permutation(sub_key, N_SEQ))(jax.random.split(first_key, N_FSDP)).astype(jnp.int32)
    recv_perm = jax.vmap(lambda sub_key: jax.random.permutation(sub_key, per_device))(jax.random.split(second_key, N_FSDP * N_SEQ))
    send_perm = jax.vmap(lambda sub_key: jax.random.permutation(sub_key, per_device))(jax.random.split(third_key, N_FSDP * N_SEQ))
    recv_perm = recv_perm.astype(jnp.int32).reshape(N_FSDP, N_SEQ * per_device)
    send_perm = send_perm.astype(jnp.int32).reshape(N_FSDP, N_SEQ * per_device)
    units = jnp.arange(per_device, dtype=jnp.int32)
    steps_back = units // capacity
    positions = jnp.arange(N_SEQ, dtype=jnp.int32)
    receiver = jnp.broadcast_to(order[:, :, None], (N_FSDP, N_SEQ, per_device))
    sender_pos = (positions[:, None] - steps_back[None, :]) % N_SEQ
    sender_pos = jnp.broadcast_to(sender_pos.reshape(1, N_SEQ * per_device), (N_FSDP, N_SEQ * per_device))
    sender = jnp.take_along_axis(order, sender_pos, axis=1).reshape(N_FSDP, N_SEQ, per_device)
    recv_index = (receiver * per_device + units[None, None, :]).reshape(N_FSDP, N_SEQ * per_device)
    send_index = (sender * per_device + units[None, None, :]).reshape(N_FSDP, N_SEQ * per_device)
    slot_local = receiver.reshape(N_FSDP, N_SEQ * per_device) * per_device + jnp.take_along_axis(recv_perm, recv_index, axis=1)
    neighbour_local = sender.reshape(N_FSDP, N_SEQ * per_device) * per_device + jnp.take_along_axis(send_perm, send_index, axis=1)
    group_base = (jnp.arange(N_FSDP, dtype=jnp.int32) * (N_SEQ * per_device))[:, None]
    rows = jnp.broadcast_to(jnp.arange(N_FSDP, dtype=jnp.int32)[:, None], (N_FSDP, N_SEQ * per_device))
    result = jnp.zeros((N_FSDP, N_SEQ * per_device), jnp.int32).at[rows, neighbour_local].set(slot_local + group_base)
    return result.reshape(N_FSDP * N_SEQ * per_device).astype(jnp.int32)


def shard_levels(stream_key, extent, shards, low, top_value):
    loudness, own = 1.0, jax.random.fold_in(stream_key, 6)
    for dim, blocks in shards:
        draws = jnp.exp(jax.random.uniform(jax.random.fold_in(own, dim), (blocks,), jnp.float32, low / len(shards), top_value / len(shards)))
        loudness = loudness * jnp.repeat(draws, extent[dim] // blocks).reshape([-1 if axis == dim else 1 for axis in range(len(extent))])
    return loudness


def gaussian(own_key, extent, width, most, cuts=(), kind=jnp.bfloat16):
    factor_of = shard_levels(own_key, extent, cuts, -0.22, 0.18) if cuts else 1.0
    array = jax.random.normal(own_key, extent, jnp.float32) * width * factor_of
    return jnp.minimum(jnp.maximum(array, -most), most).astype(kind)


def setup_inputs(seed: int = 0) -> dict:
    streams_of = jax.random.split(jax.random.key(seed), 10)
    return {
        "queries": draw_queries(jax.random.fold_in(streams_of[9], 71), 0),
        "neighbours": gaussian(streams_of[1], (NBRS * NLEN, E), 1.0, 6.0, ((0, 512),)),
        "neighbour_slot": draw_neighbour_slot(jax.random.fold_in(streams_of[9], 71), 0),
        "enc_gain": jnp.clip(1.0 + 0.18 * jax.random.normal(streams_of[3], (E,), jnp.float32), 0.1, 1.9),
        "enc_up": gaussian(streams_of[4], (E, EF), E ** -0.5, 0.1875, ((1, 64),)),
        "enc_down": gaussian(streams_of[5], (EF, E), EF ** -0.5, 0.125, ((0, 64),)),
        "key_proj": gaussian(streams_of[6], (E, HEADS * HD), E ** -0.5, 0.1875, ((1, 64),)),
        "value_proj": gaussian(streams_of[7], (E, HEADS * HD), E ** -0.5, 0.1875, ((1, 64),)),
        "grad_attn": gaussian(streams_of[8], (SPANS * CL, HEADS * HD), 1.0, 6.0, ((0, 512),)),
    }


EPS = 1e-06

def encode(raw_rows, enc_gain, enc_up, enc_down):
    floats = raw_rows.astype(jnp.float32)
    normed = (floats * lax.rsqrt(lax.optimization_barrier(jnp.mean(floats * floats, axis=-1, keepdims=True)) + EPS) * enc_gain).astype(jnp.bfloat16)
    hidden = jax.nn.gelu(jnp.dot(normed, enc_up, preferred_element_type=jnp.float32), approximate=True).astype(jnp.bfloat16)
    return (floats + jnp.dot(hidden, enc_down, preferred_element_type=jnp.float32)).astype(jnp.bfloat16)

def reference(queries, neighbours, neighbour_slot, enc_gain, enc_up, enc_down, key_proj, value_proj, grad_attn):
    per_group = N_SEQ * CH_DEV * NPC
    span_count = N_SEQ * CH_DEV
    group_ids = jnp.arange(N_FSDP, dtype=jnp.int32)
    raw_blocks = neighbours.reshape(N_FSDP, per_group * NLEN, E)
    slot_blocks = neighbour_slot.reshape(N_FSDP, per_group) - (group_ids * per_group)[:, None]
    query_blocks = queries.reshape(N_FSDP, span_count, CL, HEADS, HD)
    grad_blocks = grad_attn.reshape(N_FSDP, span_count, CL, HEADS, HD)
    score_scale = HD ** (-0.5)

    def one_group(members):
        raw_rows, slot_list, group_queries, group_grads = members
        encoded = encode(raw_rows, enc_gain, enc_up, enc_down).reshape(per_group, NLEN, E)
        placed = jnp.zeros_like(encoded).at[slot_list.astype(jnp.int32)].set(encoded).reshape(per_group * NLEN, E)
        key_rows = jnp.dot(placed, key_proj, preferred_element_type=jnp.float32).astype(jnp.bfloat16)
        value_rows = jnp.dot(placed, value_proj, preferred_element_type=jnp.float32).astype(jnp.bfloat16)
        key_heads = key_rows.reshape(span_count, NPC * NLEN, HEADS, HD).astype(jnp.float32)
        value_heads = value_rows.reshape(span_count, NPC * NLEN, HEADS, HD).astype(jnp.float32)
        query_heads = group_queries.astype(jnp.float32)
        grad_heads = group_grads.astype(jnp.float32)
        scores = jnp.einsum('cqhd,ckhd->chqk', query_heads, key_heads) * score_scale
        exponent = jnp.exp(scores - lax.optimization_barrier(jnp.max(scores, axis=-1, keepdims=True)))
        probabilities = exponent / lax.optimization_barrier(jnp.sum(exponent, axis=-1, keepdims=True))
        prob_low = probabilities.astype(jnp.bfloat16)
        attended = jnp.einsum('chqk,ckhd->cqhd', prob_low.astype(jnp.float32), value_heads).astype(jnp.bfloat16)
        grad_probs = jnp.einsum('cqhd,ckhd->chqk', grad_heads, value_heads)
        row_delta = lax.optimization_barrier(jnp.sum(probabilities * grad_probs, axis=-1, keepdims=True))
        grad_scores = (probabilities * (grad_probs - row_delta) * score_scale).astype(jnp.bfloat16)
        grad_queries = jnp.einsum('chqk,ckhd->cqhd', grad_scores.astype(jnp.float32), key_heads).astype(jnp.bfloat16)
        grad_keys = jnp.einsum('chqk,cqhd->ckhd', grad_scores.astype(jnp.float32), query_heads).astype(jnp.bfloat16)
        grad_values = jnp.einsum('chqk,cqhd->ckhd', prob_low.astype(jnp.float32), grad_heads).astype(jnp.bfloat16)
        grad_keys = grad_keys.reshape(per_group * NLEN, HEADS * HD)
        grad_values = grad_values.reshape(per_group * NLEN, HEADS * HD)
        grad_encoded = (jnp.dot(grad_keys, key_proj.T, preferred_element_type=jnp.float32) + jnp.dot(grad_values, value_proj.T, preferred_element_type=jnp.float32)).astype(jnp.bfloat16)
        return (attended, grad_queries, grad_encoded)
    attended, grad_queries, grad_encoded = lax.map(one_group, (raw_blocks, slot_blocks, query_blocks, grad_blocks))
    total_rows = N_FSDP * span_count * CL
    return (attended.reshape(total_rows, HEADS * HD), grad_queries.reshape(total_rows, HEADS * HD), grad_encoded.reshape(N_FSDP * per_group * NLEN, E))
```

```python
import jax
import jax.numpy as jnp
from jax import lax
from jax.experimental import pallas as pl
from jax.experimental.pallas import tpu as pltpu
from jax.sharding import Mesh, PartitionSpec as P

E = 896
HEADS = 16
HD = 128
CL = 64
NLEN = 64
NPC = 2
CH_DEV = 2
NZ, NX, NY, NC = 16, 4, 4, 2
PER_DEV = CH_DEV * NPC
ROWS = PER_DEV * NLEN
UNITS = 28
HALF = UNITS // 2
QUART = UNITS // 4
EPS = 1e-06
SCALE = HD ** (-0.5)
ALL = ("z", "x", "y", "c")
NT = (((1,), (1,)), ((), ()))
NN = (((1,), (0,)), ((), ()))
TN = (((0,), (0,)), ((), ()))


def dot(a, b, dims):
    return lax.dot_general(a, b, dims, preferred_element_type=jnp.float32)


def ring_pairs(step):
    pairs = []
    for x in range(NX):
        for y in range(NY):
            pairs.append(((x * NY + y) * NC, (x * NY + (y + step) % NY) * NC))
            pairs.append(((x * NY + y) * NC + 1, ((x + step) % NX * NY + y) * NC + 1))
    return pairs


def ring(rows, step):
    return lax.ppermute(rows, ("x", "y", "c"), ring_pairs(step))


def swap(rows):
    return lax.ppermute(rows, "c", [(0, 1), (1, 0)])


def send_kernel(meta, raw_ref, out_ref):
    for i in range(PER_DEV):
        out_ref[meta[PER_DEV * meta[32] + i] // PER_DEV] = raw_ref[i]


def send_blocks(meta, raw):
    return pl.pallas_call(
        send_kernel,
        out_shape=jax.ShapeDtypeStruct((NY * NC, NLEN, E), jnp.bfloat16),
        in_specs=[
            pl.BlockSpec(memory_space=pltpu.SMEM),
            pl.BlockSpec(memory_space=pltpu.VMEM),
        ],
        out_specs=pl.BlockSpec(memory_space=pltpu.VMEM),
        name="send_blocks",
    )(meta, raw)


def gelu(x):
    return 0.5 * x * (1.0 + jnp.tanh(0.7978845608028654 * (x + 0.044715 * (x * x * x))))


def encode_kernel(
    meta, recv_ref, gain_ref, o0, o1, o2, o3, o4, s0, s1, s2, s3, s4, out_ref, buf_y, buf_x, raw, sems
):
    core, y = meta[33], meta[34]
    half = NZ // 2

    def copies(pieces, buf, place, lane):
        own, left, right, far_a, far_b = pieces
        far = (place + 2) % 4
        targets = (
            (own, buf.at[place]),
            (left, buf.at[(place + 3) % 4]),
            (right, buf.at[(place + 1) % 4]),
            (far_a, buf.at[far, 0:half]),
            (far_b, buf.at[far, half:NZ]),
        )
        return [
            pltpu.make_async_copy(src, dst, sems.at[lane, i]) for i, (src, dst) in enumerate(targets)
        ]

    own, other = (o0, o1, o2, o3, o4), (s0, s1, s2, s3, s4)

    @pl.when(core == 0)
    def _():
        for copy in copies(own, buf_y, y, 0) + copies(other, buf_x, 0, 1):
            copy.start()

    @pl.when(core != 0)
    def _():
        for copy in copies(other, buf_y, y, 0) + copies(own, buf_x, 0, 1):
            copy.start()

    first = PER_DEV * meta[32]
    for n in range(NY * NC * PER_DEV):
        slot = meta[n] - first

        @pl.when((slot >= 0) & (slot < PER_DEV))
        def _():
            raw[slot] = recv_ref[n // PER_DEV]

    floats = raw[...].reshape(ROWS, E).astype(jnp.float32)
    mean = jnp.mean(floats * floats, axis=-1, keepdims=True)
    normed = (floats * lax.rsqrt(mean + EPS) * gain_ref[...]).astype(jnp.bfloat16)

    for copy in copies(own, buf_y, y, 0):
        copy.wait()
    acc = jnp.zeros((ROWS, E), jnp.float32)

    def block(acc, up, down):
        hidden = gelu(dot(normed, up, NT)).astype(jnp.bfloat16)
        return acc + dot(hidden, down, NN)

    for part in range(2):
        for z in range(0, NZ, 8):
            acc = block(
                acc,
                buf_y[part, z : z + 8].reshape(256, E),
                buf_y[part + 2, z : z + 8].reshape(256, E),
            )
    for copy in copies(own, buf_x, 0, 1):
        copy.wait()
    for part in range(4):
        acc = block(
            acc,
            buf_x[part, :, 0:16].reshape(256, E),
            buf_x[part, :, 16:32].reshape(256, E),
        )
    out_ref[...] = (floats + acc).astype(jnp.bfloat16)


def encode(meta, recv, gain, own, other):
    hbm = pl.BlockSpec(memory_space=pl.ANY)
    vmem = pl.BlockSpec(memory_space=pltpu.VMEM)
    return pl.pallas_call(
        encode_kernel,
        out_shape=jax.ShapeDtypeStruct((ROWS, E), jnp.bfloat16),
        in_specs=[pl.BlockSpec(memory_space=pltpu.SMEM), vmem, vmem] + [hbm] * 10,
        out_specs=vmem,
        scratch_shapes=[
            pltpu.VMEM((4, NZ, 32, E), jnp.bfloat16),
            pltpu.VMEM((4, NZ, 32, E), jnp.bfloat16),
            pltpu.VMEM((PER_DEV, NLEN, E), jnp.bfloat16),
            pltpu.SemaphoreType.DMA((2, 5)),
        ],
        compiler_params=pltpu.CompilerParams(vmem_limit_bytes=28 * 1024 * 1024),
        name="encode_rows",
    )(meta, recv, gain, *own, *other)


GROUP = 4
CHUNK = 4
CUT = 8
LAST = 256


def attend_kernel(enc_ref, w_hbm, q_hbm, g_hbm, att_hbm, gq_hbm, ge_ref, w, q_ref, g_ref, kv, gkv, att, gq, sems, outs):
    def fetch(i):
        return pltpu.make_async_copy(
            w_hbm.at[i * CUT : (i + 1) * CUT], w.at[i * CUT : (i + 1) * CUT], sems.at[i]
        )

    loads = [fetch(i) for i in range(2 * HEADS // CUT)]
    loads.append(pltpu.make_async_copy(q_hbm, q_ref, sems.at[len(loads)]))
    loads.append(pltpu.make_async_copy(g_hbm, g_ref, sems.at[len(loads)]))
    for copy in loads:
        copy.start()

    enc = enc_ref[...]
    for i in range(2 * HEADS // CUT):
        loads[i].wait()
        for j in range(i * CUT, (i + 1) * CUT, CHUNK):
            rows = w[j : j + CHUNK].reshape(CHUNK * HD, E)
            kv[:, j * HD : (j + CHUNK) * HD] = dot(enc, rows, NT).astype(jnp.bfloat16)
    loads[-2].wait()
    loads[-1].wait()

    shape = (CH_DEV * CL, ROWS)
    own_span = lax.broadcasted_iota(jnp.int32, shape, 0) // CL == (
        lax.broadcasted_iota(jnp.int32, shape, 1) // (NPC * NLEN)
    )
    for base in range(0, HEADS, GROUP):
        heads = range(base, base + GROUP)
        cols = [slice(h * HD, (h + 1) * HD) for h in heads]
        kcols = [slice(2 * h * HD, (2 * h + 1) * HD) for h in heads]
        vcols = [slice((2 * h + 1) * HD, (2 * h + 2) * HD) for h in heads]
        scores = [dot(q_ref[:, c], kv[:, k], NT) for c, k in zip(cols, kcols)]
        grad_probs = [dot(g_ref[:, c], kv[:, v], NT) for c, v in zip(cols, vcols)]
        scores = [jnp.where(own_span, s * SCALE, -jnp.inf) for s in scores]
        exponent = [jnp.exp(s - jnp.max(s, axis=-1, keepdims=True)) for s in scores]
        probs = [e * (1.0 / jnp.sum(e, axis=-1, keepdims=True)) for e in exponent]
        low = [p.astype(jnp.bfloat16) for p in probs]
        delta = [jnp.sum(p * gp, axis=-1, keepdims=True) for p, gp in zip(probs, grad_probs)]
        grad_scores = [
            (p * (gp - d) * SCALE).astype(jnp.bfloat16)
            for p, gp, d in zip(probs, grad_probs, delta)
        ]
        for i, (c, k, v) in enumerate(zip(cols, kcols, vcols)):
            att[:, c] = dot(low[i], kv[:, v], NN).astype(jnp.bfloat16)
            gkv[:, v] = dot(low[i], g_ref[:, c], TN).astype(jnp.bfloat16)
            gq[:, c] = dot(grad_scores[i], kv[:, k], NN).astype(jnp.bfloat16)
            gkv[:, k] = dot(grad_scores[i], q_ref[:, c], TN).astype(jnp.bfloat16)
    stores = [
        pltpu.make_async_copy(att, att_hbm, outs.at[0]),
        pltpu.make_async_copy(gq, gq_hbm, outs.at[1]),
    ]
    for copy in stores:
        copy.start()
    rows = w[...].reshape(2 * HEADS * HD, E)
    for j in range(0, E, LAST):
        wide = slice(j, min(j + LAST, E))
        ge_ref[:, wide] = dot(gkv[...], rows[:, wide], NN).astype(jnp.bfloat16)
    for copy in stores:
        copy.wait()


def attend(enc, weights, queries, grads):
    tokens = CH_DEV * CL
    hbm = pl.BlockSpec(memory_space=pltpu.HBM)
    vmem = pl.BlockSpec(memory_space=pltpu.VMEM)
    wide = jax.ShapeDtypeStruct((tokens, HEADS * HD), jnp.bfloat16)
    full = pltpu.VMEM((tokens, HEADS * HD), jnp.bfloat16)
    both = pltpu.VMEM((ROWS, 2 * HEADS * HD), jnp.bfloat16)
    return pl.pallas_call(
        attend_kernel,
        out_shape=(wide, wide, jax.ShapeDtypeStruct((ROWS, E), jnp.bfloat16)),
        in_specs=[vmem, hbm, hbm, hbm],
        out_specs=(hbm, hbm, vmem),
        scratch_shapes=[
            pltpu.VMEM((2 * HEADS, HD, E), jnp.bfloat16),
            full,
            full,
            both,
            both,
            full,
            full,
            pltpu.SemaphoreType.DMA((2 * HEADS // CUT + 2,)),
            pltpu.SemaphoreType.DMA((2,)),
        ],
        compiler_params=pltpu.CompilerParams(vmem_limit_bytes=56 * 1024 * 1024),
        name="attend_spans",
    )(enc, weights, queries, grads)


def body(queries, neighbours, slots, gain, up, down, key_proj, value_proj, grads):
    z, x, y, c = (lax.axis_index(name) for name in ALL)
    group = NY * NC * PER_DEV
    place = jnp.stack([y * NC + c, c, y, x]).astype(jnp.int32)
    meta = jnp.concatenate([slots - (z * NX + x) * group, place])

    up = up.T
    kv_unit = jnp.where(c == 0, key_proj.T, value_proj.T)
    halves = jnp.concatenate([up[:HALF], down[:HALF]])
    quarter = jnp.pad(lax.dynamic_slice_in_dim(halves, y * QUART, QUART), ((0, 1), (0, 0)))
    pad = ((0, 16 - HALF), (0, 0))
    whole = jnp.concatenate([jnp.pad(up[HALF:], pad), jnp.pad(down[HALF:], pad)])

    along_x = lax.all_gather(jnp.concatenate([kv_unit, quarter]), "x", axis=0, tiled=False)
    kv_head = along_x[:, :32].reshape(HD, E)
    weights = lax.all_gather(kv_head, ("z", "c"), axis=0, tiled=False)

    outgoing = send_blocks(meta, neighbours.reshape(PER_DEV, NLEN, E))
    ff_unit = jnp.where(c == 0, along_x[:, 32:].reshape(32, E), whole)
    ff_unit, outgoing = lax.optimization_barrier((ff_unit, outgoing))
    recv = lax.all_to_all(outgoing, ("y", "c"), 0, 0, tiled=True)
    own = lax.all_gather(ff_unit, "z", axis=0, tiled=False)
    own, recv = lax.optimization_barrier((own, recv))
    left = ring(own, 1)
    right = ring(own, -1)
    far_a = ring(left[: NZ // 2], 1)
    far_b = ring(right[NZ // 2 :], -1)
    pieces = (own, left, right, far_a, far_b)
    others = tuple(swap(piece) for piece in pieces)

    enc = encode(meta, recv, gain.reshape(1, E), pieces, others)
    return attend(enc, weights, queries, grads)


def solution(mesh):
    wide = Mesh(mesh.devices.reshape(NZ, NX, NY, NC), ALL)
    rows = P(ALL, None)
    fsdp = ("z", "x")
    in_specs = (
        rows,
        rows,
        P(fsdp),
        P(),
        P(None, fsdp),
        P(fsdp, None),
        P(None, fsdp),
        P(None, fsdp),
        rows,
    )
    return jax.shard_map(
        body, mesh=wide, in_specs=in_specs, out_specs=(rows, rows, rows), check_vma=False
    )
```

```python
import jax
import jax.numpy as jnp
from jax import lax
from jax.experimental import pallas as pl
from jax.experimental.pallas import tpu as pltpu
from jax.sharding import Mesh, PartitionSpec as P

E = 896
HEADS = 16
HD = 128
CL = 64
NLEN = 64
NPC = 2
CH_DEV = 2
NZ, NX, NY, NC = 16, 4, 4, 2
PER_DEV = CH_DEV * NPC
ROWS = PER_DEV * NLEN
UNITS = 28
HALF = UNITS // 2
QUART = UNITS // 4
EPS = 1e-06
SCALE = HD ** (-0.5)
ALL = ("z", "x", "y", "c")
NT = (((1,), (1,)), ((), ()))
NN = (((1,), (0,)), ((), ()))
TN = (((0,), (0,)), ((), ()))


def dot(a, b, dims):
    return lax.dot_general(a, b, dims, preferred_element_type=jnp.float32)


def ring_pairs(step):
    pairs = []
    for x in range(NX):
        for y in range(NY):
            pairs.append(((x * NY + y) * NC, (x * NY + (y + step) % NY) * NC))
            pairs.append(((x * NY + y) * NC + 1, ((x + step) % NX * NY + y) * NC + 1))
    return pairs


def ring(rows, step):
    return lax.ppermute(rows, ("x", "y", "c"), ring_pairs(step))


def swap(rows):
    return lax.ppermute(rows, "c", [(0, 1), (1, 0)])


def send_kernel(meta, raw_ref, out_ref):
    for i in range(PER_DEV):
        out_ref[meta[PER_DEV * meta[32] + i] // PER_DEV] = raw_ref[i]


def send_blocks(meta, raw):
    return pl.pallas_call(
        send_kernel,
        out_shape=jax.ShapeDtypeStruct((NY * NC, NLEN, E), jnp.bfloat16),
        in_specs=[
            pl.BlockSpec(memory_space=pltpu.SMEM),
            pl.BlockSpec(memory_space=pltpu.VMEM),
        ],
        out_specs=pl.BlockSpec(memory_space=pltpu.VMEM),
        compiler_params=pltpu.CompilerParams(vmem_limit_bytes=8 * 1024 * 1024),
        name="send_blocks",
    )(meta, raw)


def gelu(x):
    return 0.5 * x * (1.0 + jnp.tanh(0.7978845608028654 * (x + 0.044715 * (x * x * x))))


def place_kernel(meta, recv_ref, gain_ref, raw_ref, normed_ref):
    first = PER_DEV * meta[32]
    for n in range(NY * NC * PER_DEV):
        slot = meta[n] - first

        @pl.when((slot >= 0) & (slot < PER_DEV))
        def _():
            raw_ref[slot] = recv_ref[n // PER_DEV]

    floats = raw_ref[...].astype(jnp.float32)
    mean = jnp.mean(floats * floats, axis=-1, keepdims=True)
    normed_ref[...] = (floats * lax.rsqrt(mean + EPS) * gain_ref[...]).astype(jnp.bfloat16)


def place(meta, recv, gain):
    vmem = pl.BlockSpec(memory_space=pltpu.VMEM)
    rows = jax.ShapeDtypeStruct((PER_DEV, NLEN, E), jnp.bfloat16)
    return pl.pallas_call(
        place_kernel,
        out_shape=(rows, rows),
        in_specs=[pl.BlockSpec(memory_space=pltpu.SMEM), vmem, vmem],
        out_specs=(vmem, vmem),
        compiler_params=pltpu.CompilerParams(vmem_limit_bytes=8 * 1024 * 1024),
        name="place_rows",
    )(meta, recv, gain)


def both_cores(mine, other):
    return jnp.concatenate([mine[...].reshape(ROWS, E), other[...].reshape(ROWS, E)])


def blocks_y(pairs):
    return [(up[...].reshape(256, E), down[...].reshape(256, E)) for up, down in pairs]


def blocks_x(pieces):
    out = []
    for one, two in zip(pieces[::2], pieces[1::2]):
        ups, downs = [], []
        for piece in (one, two):
            ups.append(piece[:, 0:16].reshape(128, E))
            downs.append(piece[:, 16:32].reshape(128, E))
        out.append((jnp.concatenate(ups), jnp.concatenate(downs)))
    return out


def multiply(normed, blocks):
    total = None
    for up, down in blocks:
        hidden = gelu(dot(normed, up, NT)).astype(jnp.bfloat16)
        part = dot(hidden, down, NN)
        total = part if total is None else total + part
    return total


def by_case(meta, even, odd, x_pieces, write):
    core, parity = meta[33], meta[34] % 2

    @pl.when((core == 0) & (parity == 0))
    def _():
        write(blocks_y(even))

    @pl.when((core == 0) & (parity == 1))
    def _():
        write(blocks_y(odd))

    @pl.when(core != 0)
    def _():
        write(blocks_x(x_pieces))


def early_kernel(meta, mine, other, own_a, own_b, left_a, left_b, right_a, right_b, acc_ref):
    normed = both_cores(mine, other)

    def write(blocks):
        acc_ref[...] = multiply(normed, blocks)

    by_case(
        meta,
        ((own_a, right_a), (own_b, right_b)),
        ((left_a, own_a), (left_b, own_b)),
        (own_a, own_b, left_a, left_b, right_a, right_b),
        write,
    )


def late_kernel(
    meta, mine, other, acc, left_a, left_b, right_a, right_b, far_a, far_b, mine_ref, other_ref
):
    normed = both_cores(mine, other)

    def write(blocks):
        total = acc[...] + multiply(normed, blocks)
        mine_ref[...] = total[:ROWS]
        other_ref[...] = total[ROWS:]

    by_case(
        meta,
        ((far_a, left_a), (far_b, left_b)),
        ((right_a, far_a), (right_b, far_b)),
        (far_a, far_b),
        write,
    )


def encode_part(kernel, outs, meta, *arrays):
    vmem = pl.BlockSpec(memory_space=pltpu.VMEM)
    return pl.pallas_call(
        kernel,
        out_shape=outs,
        in_specs=[pl.BlockSpec(memory_space=pltpu.SMEM)] + [vmem] * len(arrays),
        out_specs=jax.tree.map(lambda _: vmem, outs),
        compiler_params=pltpu.CompilerParams(vmem_limit_bytes=28 * 1024 * 1024),
        name=kernel.__name__,
    )(meta, *arrays)


GROUP = 4
CHUNK = 4
CUT = 2 * GROUP
LAST = 256
LIMIT = 48 * 1024 * 1024


def attend_kernel(
    raw_ref, mine_ref, other_ref, w_hbm, q_hbm, g_hbm, att_hbm, gq_hbm, ge_ref, w, q_ref, g_ref, kv, gkv, att, gq, sems, outs
):
    def fetch(i):
        return pltpu.make_async_copy(
            w_hbm.at[i * CUT : (i + 1) * CUT], w.at[i * CUT : (i + 1) * CUT], sems.at[i]
        )

    loads = [fetch(i) for i in range(2 * HEADS // CUT)]
    loads.append(pltpu.make_async_copy(q_hbm, q_ref, sems.at[len(loads)]))
    loads.append(pltpu.make_async_copy(g_hbm, g_ref, sems.at[len(loads)]))
    for copy in loads:
        copy.start()

    floats = raw_ref[...].reshape(ROWS, E).astype(jnp.float32)
    enc = (floats + (mine_ref[...] + other_ref[...])).astype(jnp.bfloat16)
    first = lax.broadcasted_iota(jnp.int32, (NPC * NLEN, CH_DEV * CL), 1) < CL
    half = NPC * NLEN

    def fold(full):
        return jnp.where(first, full[:half], full[half:])

    def spread(part):
        zero = jnp.zeros_like(part)
        return jnp.concatenate([jnp.where(first, part, zero), jnp.where(first, zero, part)])

    for base in range(0, HEADS, GROUP):
        loads[base // GROUP].wait()
        for j in range(2 * base, 2 * (base + GROUP), CHUNK):
            rows = w[j : j + CHUNK].reshape(CHUNK * HD, E)
            kv[:, j * HD : (j + CHUNK) * HD] = dot(enc, rows, NT).astype(jnp.bfloat16)
        if base == 0:
            loads[-2].wait()
            loads[-1].wait()
        heads = range(base, base + GROUP)
        cols = [slice(h * HD, (h + 1) * HD) for h in heads]
        kcols = [slice(2 * h * HD, (2 * h + 1) * HD) for h in heads]
        vcols = [slice((2 * h + 1) * HD, (2 * h + 2) * HD) for h in heads]
        scores = [fold(dot(kv[:, k], q_ref[:, c], NT)) * SCALE for c, k in zip(cols, kcols)]
        grad_probs = [fold(dot(kv[:, v], g_ref[:, c], NT)) for c, v in zip(cols, vcols)]
        exponent = [jnp.exp(s - jnp.max(s, axis=0, keepdims=True)) for s in scores]
        probs = [e * (1.0 / jnp.sum(e, axis=0, keepdims=True)) for e in exponent]
        delta = [jnp.sum(p * gp, axis=0, keepdims=True) for p, gp in zip(probs, grad_probs)]
        low = [spread(p).astype(jnp.bfloat16) for p in probs]
        grad_scores = [
            spread(p * (gp - d) * SCALE).astype(jnp.bfloat16)
            for p, gp, d in zip(probs, grad_probs, delta)
        ]
        for i, (c, k, v) in enumerate(zip(cols, kcols, vcols)):
            att[:, c] = dot(low[i], kv[:, v], TN).astype(jnp.bfloat16)
            gkv[:, v] = dot(low[i], g_ref[:, c], NN).astype(jnp.bfloat16)
            gq[:, c] = dot(grad_scores[i], kv[:, k], TN).astype(jnp.bfloat16)
            gkv[:, k] = dot(grad_scores[i], q_ref[:, c], NN).astype(jnp.bfloat16)
    stores = [
        pltpu.make_async_copy(att, att_hbm, outs.at[0]),
        pltpu.make_async_copy(gq, gq_hbm, outs.at[1]),
    ]
    for copy in stores:
        copy.start()
    rows = w[...].reshape(2 * HEADS * HD, E)
    for j in range(0, E, LAST):
        wide = slice(j, min(j + LAST, E))
        ge_ref[:, wide] = dot(gkv[...], rows[:, wide], NN).astype(jnp.bfloat16)
    for copy in stores:
        copy.wait()


def attend(raw, mine, other, weights, queries, grads):
    tokens = CH_DEV * CL
    hbm = pl.BlockSpec(memory_space=pltpu.HBM)
    vmem = pl.BlockSpec(memory_space=pltpu.VMEM)
    wide = jax.ShapeDtypeStruct((tokens, HEADS * HD), jnp.bfloat16)
    full = pltpu.VMEM((tokens, HEADS * HD), jnp.bfloat16)
    both = pltpu.VMEM((ROWS, 2 * HEADS * HD), jnp.bfloat16)
    return pl.pallas_call(
        attend_kernel,
        out_shape=(wide, wide, jax.ShapeDtypeStruct((ROWS, E), jnp.bfloat16)),
        in_specs=[vmem, vmem, vmem, hbm, hbm, hbm],
        out_specs=(hbm, hbm, vmem),
        scratch_shapes=[
            pltpu.VMEM((2 * HEADS, HD, E), jnp.bfloat16),
            full,
            full,
            both,
            both,
            full,
            full,
            pltpu.SemaphoreType.DMA((2 * HEADS // CUT + 2,)),
            pltpu.SemaphoreType.DMA((2,)),
        ],
        compiler_params=pltpu.CompilerParams(vmem_limit_bytes=LIMIT),
        name="attend_spans",
    )(raw, mine, other, weights, queries, grads)


def body(queries, neighbours, slots, gain, up, down, key_proj, value_proj, grads):
    z, x, y, c = (lax.axis_index(name) for name in ALL)
    group = NY * NC * PER_DEV
    here = jnp.stack([y * NC + c, c, y, x]).astype(jnp.int32)
    meta = jnp.concatenate([slots - (z * NX + x) * group, here])

    up = up.T
    kv_unit = jnp.where(c == 0, key_proj.T, value_proj.T)
    halves = jnp.concatenate([up[:QUART], down[:QUART], up[QUART:HALF], down[QUART:HALF]])
    quarter = jnp.pad(lax.dynamic_slice_in_dim(halves, y * QUART, QUART), ((0, 1), (0, 0)))
    pad = ((0, 16 - HALF), (0, 0))
    whole = jnp.concatenate([jnp.pad(up[HALF:], pad), jnp.pad(down[HALF:], pad)])

    along_x = lax.all_gather(jnp.concatenate([kv_unit, quarter]), "x", axis=0, tiled=False)
    kv_head = along_x[:, :32].reshape(HD, E)
    weights = lax.all_gather(kv_head, ("z", "c"), axis=0, tiled=False)

    outgoing = send_blocks(meta, neighbours.reshape(PER_DEV, NLEN, E))
    ff_unit = jnp.where(c == 0, along_x[:, 32:].reshape(32, E), whole)
    ff_unit, outgoing = lax.optimization_barrier((ff_unit, outgoing))
    recv = lax.all_to_all(outgoing, ("y", "c"), 0, 0, tiled=True)
    own = lax.all_gather(ff_unit, "z", axis=0, tiled=False)
    own, recv = lax.optimization_barrier((own, recv))
    raw, normed = place(meta, recv, gain.reshape(1, E))
    other = swap(normed)
    own_a, own_b = own[: NZ // 2], own[NZ // 2 :]
    left_a, right_b = ring(own_a, 1), ring(own_b, -1)
    left_b, right_a = ring(own_b, 1), ring(own_a, -1)
    far_a, far_b = ring(left_a, 1), ring(right_b, -1)
    near = (left_a, left_b, right_a, right_b)
    one = jax.ShapeDtypeStruct((ROWS, E), jnp.float32)
    two = jax.ShapeDtypeStruct((2 * ROWS, E), jnp.float32)
    acc = encode_part(early_kernel, two, meta, normed, other, own_a, own_b, *near)
    mine, given = encode_part(
        late_kernel, (one, one), meta, normed, other, acc, *near, far_a, far_b
    )
    return attend(raw, mine, swap(given), weights, queries, grads)


def solution(mesh):
    wide = Mesh(mesh.devices.reshape(NZ, NX, NY, NC), ALL)
    rows = P(ALL, None)
    fsdp = ("z", "x")
    in_specs = (
        rows,
        rows,
        P(fsdp),
        P(),
        P(None, fsdp),
        P(fsdp, None),
        P(None, fsdp),
        P(None, fsdp),
        rows,
    )
    return jax.shard_map(
        body, mesh=wide, in_specs=in_specs, out_specs=(rows, rows, rows), check_vma=False
    )
```

```python
import jax
import jax.numpy as jnp
from jax import lax
from jax.experimental import pallas as pl
from jax.experimental.pallas import tpu as pltpu
from jax.sharding import Mesh, PartitionSpec as P

E = 896
HEADS = 16
HD = 128
CL = 64
NLEN = 64
NPC = 2
CH_DEV = 2
NZ, NX, NY, NC = 16, 4, 4, 2
PER_DEV = CH_DEV * NPC
ROWS = PER_DEV * NLEN
UNITS = 28
HALF = UNITS // 2
QUART = UNITS // 4
EPS = 1e-06
SCALE = HD ** (-0.5)
ALL = ("z", "x", "y", "c")
NT = (((1,), (1,)), ((), ()))
NN = (((1,), (0,)), ((), ()))
TN = (((0,), (0,)), ((), ()))


def dot(a, b, dims):
    return lax.dot_general(a, b, dims, preferred_element_type=jnp.float32)


def ring_pairs(step):
    pairs = []
    for x in range(NX):
        for y in range(NY):
            pairs.append(((x * NY + y) * NC, (x * NY + (y + step) % NY) * NC))
            pairs.append(((x * NY + y) * NC + 1, ((x + step) % NX * NY + y) * NC + 1))
    return pairs


def ring(rows, step):
    return lax.ppermute(rows, ("x", "y", "c"), ring_pairs(step))


def swap(rows):
    return lax.ppermute(rows, "c", [(0, 1), (1, 0)])


def send_kernel(meta, raw_ref, out_ref, sems):
    copies = []
    for i in range(PER_DEV):
        target = meta[PER_DEV * meta[32] + i] // PER_DEV
        copies.append(pltpu.make_async_copy(raw_ref.at[i], out_ref.at[target], sems.at[i]))
    for copy in copies:
        copy.start()
    for copy in copies:
        copy.wait()


def send_blocks(meta, raw):
    hbm = pl.BlockSpec(memory_space=pl.ANY)
    return pl.pallas_call(
        send_kernel,
        out_shape=jax.ShapeDtypeStruct((NY * NC, NLEN, E), jnp.bfloat16),
        in_specs=[pl.BlockSpec(memory_space=pltpu.SMEM), hbm],
        out_specs=hbm,
        scratch_shapes=[pltpu.SemaphoreType.DMA((PER_DEV,))],
        compiler_params=pltpu.CompilerParams(vmem_limit_bytes=56 * 1024 * 1024),
        name="send_blocks",
    )(meta, raw)


def units_kernel(spot, key_ref, value_ref, up_ref, down_ref, unit_ref, whole_ref):
    core, y = spot[0] % 2, spot[0] // 2 % NY

    def pick(ref, count, start, rows, offset, length):
        to = lax.broadcasted_iota(jnp.int32, (count, rows), 0) - offset
        source = lax.broadcasted_iota(jnp.int32, (count, rows), 1) - start
        hot = (to == source) & (to >= 0) & (to < length)
        return dot(hot.astype(jnp.float32).astype(jnp.bfloat16), ref[...], NN)

    def only(condition, value):
        return jnp.where(condition, value, 0)

    side = QUART * (y // 2)
    quarter = pick(up_ref, 40, side, UNITS, 32, only(y % 2 == 0, QUART)) + pick(
        down_ref, 40, side, UNITS, 32, only(y % 2 == 1, QUART)
    )
    rows = pick(key_ref, 40, 0, 32, 0, only(core == 0, 32)) + pick(
        value_ref, 40, 0, 32, 0, only(core == 1, 32)
    )
    unit_ref[...] = (rows + quarter).astype(jnp.bfloat16)
    whole_ref[...] = (
        pick(up_ref, 32, HALF, UNITS, 0, HALF) + pick(down_ref, 32, HALF, UNITS, 16, HALF)
    ).astype(jnp.bfloat16)


def units(spot, key_rows, value_rows, up_rows, down_rows):
    vmem = pl.BlockSpec(memory_space=pltpu.VMEM)
    return pl.pallas_call(
        units_kernel,
        out_shape=(
            jax.ShapeDtypeStruct((40, E), jnp.bfloat16),
            jax.ShapeDtypeStruct((32, E), jnp.bfloat16),
        ),
        in_specs=[pl.BlockSpec(memory_space=pltpu.SMEM)] + [vmem] * 4,
        out_specs=(vmem, vmem),
        compiler_params=pltpu.CompilerParams(vmem_limit_bytes=56 * 1024 * 1024),
        name="pick_units",
    )(spot, key_rows, value_rows, up_rows, down_rows)


def gelu(x):
    return 0.5 * x * (1.0 + jnp.tanh(0.7978845608028654 * (x + 0.044715 * (x * x * x))))


def place_kernel(meta, recv_ref, gain_ref, raw_ref, normed_ref):
    first = PER_DEV * meta[32]
    for n in range(NY * NC * PER_DEV):
        slot = meta[n] - first

        @pl.when((slot >= 0) & (slot < PER_DEV))
        def _():
            raw_ref[slot] = recv_ref[n // PER_DEV]

    floats = raw_ref[...].astype(jnp.float32)
    mean = jnp.mean(floats * floats, axis=-1, keepdims=True)
    normed_ref[...] = (floats * lax.rsqrt(mean + EPS) * gain_ref[...]).astype(jnp.bfloat16)


def place(meta, recv, gain):
    vmem = pl.BlockSpec(memory_space=pltpu.VMEM)
    rows = jax.ShapeDtypeStruct((PER_DEV, NLEN, E), jnp.bfloat16)
    return pl.pallas_call(
        place_kernel,
        out_shape=(rows, rows),
        in_specs=[pl.BlockSpec(memory_space=pltpu.SMEM), vmem, vmem],
        out_specs=(vmem, vmem),
        compiler_params=pltpu.CompilerParams(vmem_limit_bytes=8 * 1024 * 1024),
        name="place_rows",
    )(meta, recv, gain)


def both_cores(mine, other):
    return jnp.concatenate([mine[...].reshape(ROWS, E), other[...].reshape(ROWS, E)])


def blocks_y(pairs):
    return [(up[...].reshape(256, E), down[...].reshape(256, E)) for up, down in pairs]


def blocks_x(pieces):
    out = []
    for one, two in zip(pieces[::2], pieces[1::2]):
        ups, downs = [], []
        for piece in (one, two):
            ups.append(piece[:, 0:16].reshape(128, E))
            downs.append(piece[:, 16:32].reshape(128, E))
        out.append((jnp.concatenate(ups), jnp.concatenate(downs)))
    return out


def multiply(normed, blocks):
    total = None
    for up, down in blocks:
        hidden = gelu(dot(normed, up, NT)).astype(jnp.bfloat16)
        part = dot(hidden, down, NN)
        total = part if total is None else total + part
    return total


def by_case(meta, even, odd, x_pieces, write):
    core, parity = meta[33], meta[34] % 2

    @pl.when((core == 0) & (parity == 0))
    def _():
        write(blocks_y(even))

    @pl.when((core == 0) & (parity == 1))
    def _():
        write(blocks_y(odd))

    @pl.when(core != 0)
    def _():
        write(blocks_x(x_pieces))


def early_kernel(meta, mine, other, own_a, own_b, left_a, left_b, right_a, right_b, acc_ref):
    normed = both_cores(mine, other)

    def write(blocks):
        acc_ref[...] = multiply(normed, blocks)

    by_case(
        meta,
        ((own_a, right_a), (own_b, right_b)),
        ((left_a, own_a), (left_b, own_b)),
        (own_a, own_b, left_a, left_b, right_a, right_b),
        write,
    )


def late_kernel(
    meta, raw, mine, other, acc, left_a, left_b, right_a, right_b, far_a, far_b, mine_ref, other_ref
):
    normed = both_cores(mine, other)

    def write(blocks):
        total = acc[...] + multiply(normed, blocks)
        mine_ref[...] = total[:ROWS] + raw[...].reshape(ROWS, E).astype(jnp.float32)
        other_ref[...] = total[ROWS:]

    by_case(
        meta,
        ((far_a, left_a), (far_b, left_b)),
        ((right_a, far_a), (right_b, far_b)),
        (far_a, far_b),
        write,
    )


def encode_part(kernel, outs, meta, *arrays):
    vmem = pl.BlockSpec(memory_space=pltpu.VMEM)
    return pl.pallas_call(
        kernel,
        out_shape=outs,
        in_specs=[pl.BlockSpec(memory_space=pltpu.SMEM)] + [vmem] * len(arrays),
        out_specs=jax.tree.map(lambda _: vmem, outs),
        compiler_params=pltpu.CompilerParams(vmem_limit_bytes=14 * 1024 * 1024),
        name=kernel.__name__,
    )(meta, *arrays)


GROUP = 4
CHUNK = 4
CUT = 2 * GROUP
LAST = 256
LIMIT = 48 * 1024 * 1024


def attend_kernel(
    mine_ref, other_ref, w_hbm, q_hbm, g_hbm, att_hbm, gq_hbm, ge_ref, w, q_ref, g_ref, kv, gkv, att, gq, sems, outs
):
    def fetch(i):
        return pltpu.make_async_copy(
            w_hbm.at[i * CUT : (i + 1) * CUT], w.at[i * CUT : (i + 1) * CUT], sems.at[i]
        )

    loads = [fetch(i) for i in range(2 * HEADS // CUT)]
    loads.append(pltpu.make_async_copy(q_hbm, q_ref, sems.at[len(loads)]))
    loads.append(pltpu.make_async_copy(g_hbm, g_ref, sems.at[len(loads)]))
    for copy in loads:
        copy.start()

    enc = (mine_ref[...] + other_ref[...]).astype(jnp.bfloat16)
    first = lax.broadcasted_iota(jnp.int32, (NPC * NLEN, CH_DEV * CL), 1) < CL
    half = NPC * NLEN

    def fold(full):
        return jnp.where(first, full[:half], full[half:])

    def spread(part):
        zero = jnp.zeros_like(part)
        return jnp.concatenate([jnp.where(first, part, zero), jnp.where(first, zero, part)])

    for base in range(0, HEADS, GROUP):
        loads[base // GROUP].wait()
        for j in range(2 * base, 2 * (base + GROUP), CHUNK):
            rows = w[j : j + CHUNK].reshape(CHUNK * HD, E)
            kv[:, j * HD : (j + CHUNK) * HD] = dot(enc, rows, NT).astype(jnp.bfloat16)
        if base == 0:
            loads[-2].wait()
            loads[-1].wait()
        heads = range(base, base + GROUP)
        cols = [slice(h * HD, (h + 1) * HD) for h in heads]
        kcols = [slice(2 * h * HD, (2 * h + 1) * HD) for h in heads]
        vcols = [slice((2 * h + 1) * HD, (2 * h + 2) * HD) for h in heads]
        scores = [fold(dot(kv[:, k], q_ref[:, c], NT)) * SCALE for c, k in zip(cols, kcols)]
        grad_probs = [fold(dot(kv[:, v], g_ref[:, c], NT)) for c, v in zip(cols, vcols)]
        exponent = [jnp.exp(s - jnp.max(s, axis=0, keepdims=True)) for s in scores]
        probs = [e * (1.0 / jnp.sum(e, axis=0, keepdims=True)) for e in exponent]
        delta = [jnp.sum(p * gp, axis=0, keepdims=True) for p, gp in zip(probs, grad_probs)]
        low = [spread(p).astype(jnp.bfloat16) for p in probs]
        grad_scores = [
            spread(p * (gp - d) * SCALE).astype(jnp.bfloat16)
            for p, gp, d in zip(probs, grad_probs, delta)
        ]
        for i, (c, k, v) in enumerate(zip(cols, kcols, vcols)):
            att[:, c] = dot(low[i], kv[:, v], TN).astype(jnp.bfloat16)
            gkv[:, v] = dot(low[i], g_ref[:, c], NN).astype(jnp.bfloat16)
            gq[:, c] = dot(grad_scores[i], kv[:, k], TN).astype(jnp.bfloat16)
            gkv[:, k] = dot(grad_scores[i], q_ref[:, c], NN).astype(jnp.bfloat16)
    stores = [
        pltpu.make_async_copy(att, att_hbm, outs.at[0]),
        pltpu.make_async_copy(gq, gq_hbm, outs.at[1]),
    ]
    for copy in stores:
        copy.start()
    rows = w[...].reshape(2 * HEADS * HD, E)
    for j in range(0, E, LAST):
        wide = slice(j, min(j + LAST, E))
        ge_ref[:, wide] = dot(gkv[...], rows[:, wide], NN).astype(jnp.bfloat16)
    for copy in stores:
        copy.wait()


def attend(mine, other, weights, queries, grads):
    tokens = CH_DEV * CL
    hbm = pl.BlockSpec(memory_space=pltpu.HBM)
    vmem = pl.BlockSpec(memory_space=pltpu.VMEM)
    wide = jax.ShapeDtypeStruct((tokens, HEADS * HD), jnp.bfloat16)
    full = pltpu.VMEM((tokens, HEADS * HD), jnp.bfloat16)
    both = pltpu.VMEM((ROWS, 2 * HEADS * HD), jnp.bfloat16)
    return pl.pallas_call(
        attend_kernel,
        out_shape=(wide, wide, jax.ShapeDtypeStruct((ROWS, E), jnp.bfloat16)),
        in_specs=[vmem, vmem, hbm, hbm, hbm],
        out_specs=(hbm, hbm, vmem),
        scratch_shapes=[
            pltpu.VMEM((2 * HEADS, HD, E), jnp.bfloat16),
            full,
            full,
            both,
            both,
            full,
            full,
            pltpu.SemaphoreType.DMA((2 * HEADS // CUT + 2,)),
            pltpu.SemaphoreType.DMA((2,)),
        ],
        compiler_params=pltpu.CompilerParams(vmem_limit_bytes=LIMIT),
        name="attend_spans",
    )(mine, other, weights, queries, grads)


def body(queries, neighbours, slots, gain, up, down, key_proj, value_proj, grads):
    z, x, y, c = (lax.axis_index(name) for name in ALL)
    group = NY * NC * PER_DEV
    here = jnp.stack([y * NC + c, c, y, x]).astype(jnp.int32)
    meta = jnp.concatenate([slots - (z * NX + x) * group, here])

    spot = (y * NC + c).astype(jnp.int32).reshape(1)
    unit, whole = units(spot, key_proj.T, value_proj.T, up.T, down)
    along_x = lax.all_gather(unit, "x", axis=0, tiled=False)
    kv_head = along_x[:, :32].reshape(HD, E)
    weights = lax.all_gather(kv_head, ("z", "c"), axis=0, tiled=False)

    ff_unit = jnp.where(c == 0, along_x[:, 32:].reshape(32, E), whole)
    own = lax.all_gather(ff_unit, "z", axis=0, tiled=False)
    own, rows = lax.optimization_barrier((own, neighbours))
    outgoing = send_blocks(meta, rows.reshape(PER_DEV, NLEN, E))
    recv = lax.all_to_all(outgoing, ("y", "c"), 0, 0, tiled=True)
    raw, normed = place(meta, recv, gain.reshape(1, E))
    other = swap(normed)
    own_a, own_b = own[: NZ // 2], own[NZ // 2 :]
    left_a, right_b = ring(own_a, 1), ring(own_b, -1)
    left_b, right_a = ring(own_b, 1), ring(own_a, -1)
    far_a, far_b = ring(left_a, 1), ring(right_b, -1)
    near = (left_a, left_b, right_a, right_b)
    one = jax.ShapeDtypeStruct((ROWS, E), jnp.float32)
    two = jax.ShapeDtypeStruct((2 * ROWS, E), jnp.float32)
    acc = encode_part(early_kernel, two, meta, normed, other, own_a, own_b, *near)
    mine, given = encode_part(
        late_kernel, (one, one), meta, raw, normed, other, acc, *near, far_a, far_b
    )
    return attend(mine, swap(given), weights, queries, grads)


def solution(mesh):
    wide = Mesh(mesh.devices.reshape(NZ, NX, NY, NC), ALL)
    rows = P(ALL, None)
    fsdp = ("z", "x")
    in_specs = (
        rows,
        rows,
        P(fsdp),
        P(),
        P(None, fsdp),
        P(fsdp, None),
        P(None, fsdp),
        P(None, fsdp),
        rows,
    )
    return jax.shard_map(
        body, mesh=wide, in_specs=in_specs, out_specs=(rows, rows, rows), check_vma=False
    )
```

```python
import jax
import jax.numpy as jnp
from jax import lax
from jax.experimental import pallas as pl
from jax.experimental.pallas import tpu as pltpu
from jax.sharding import Mesh, PartitionSpec as P

E = 896
HEADS = 16
HD = 128
CL = 64
NLEN = 64
NPC = 2
CH_DEV = 2
NZ, NX, NY, NC = 16, 4, 4, 2
PER_DEV = CH_DEV * NPC
ROWS = PER_DEV * NLEN
UNITS = 28
HALF = UNITS // 2
QUART = UNITS // 4
EPS = 1e-06
SCALE = HD ** (-0.5)
ALL = ("z", "x", "y", "c")
NT = (((1,), (1,)), ((), ()))
NN = (((1,), (0,)), ((), ()))
TN = (((0,), (0,)), ((), ()))


def dot(a, b, dims):
    return lax.dot_general(a, b, dims, preferred_element_type=jnp.float32)


def ring_pairs(step):
    pairs = []
    for x in range(NX):
        for y in range(NY):
            pairs.append(((x * NY + y) * NC, (x * NY + (y + step) % NY) * NC))
            pairs.append(((x * NY + y) * NC + 1, ((x + step) % NX * NY + y) * NC + 1))
    return pairs


def ring(rows, step):
    return lax.ppermute(rows, ("x", "y", "c"), ring_pairs(step))


def swap(rows):
    return lax.ppermute(rows, "c", [(0, 1), (1, 0)])


def send_kernel(meta, raw_ref, out_ref):
    for i in range(PER_DEV):
        out_ref[meta[PER_DEV * meta[32] + i] // PER_DEV] = raw_ref[i]


def send_blocks(meta, raw):
    vmem = pl.BlockSpec(memory_space=pltpu.VMEM)
    return pl.pallas_call(
        send_kernel,
        out_shape=jax.ShapeDtypeStruct((NY * NC, NLEN, E), jnp.bfloat16),
        in_specs=[pl.BlockSpec(memory_space=pltpu.SMEM), vmem],
        out_specs=vmem,
        compiler_params=pltpu.CompilerParams(vmem_limit_bytes=8 * 1024 * 1024),
        name="send_blocks",
    )(meta, raw)


def units_kernel(spot, key_ref, value_ref, up_ref, down_ref, unit_ref, whole_ref):
    core, y = spot[0] % 2, spot[0] // 2 % NY

    def pick(ref, count, start, rows, offset, length):
        to = lax.broadcasted_iota(jnp.int32, (count, rows), 0) - offset
        source = lax.broadcasted_iota(jnp.int32, (count, rows), 1) - start
        hot = (to == source) & (to >= 0) & (to < length)
        return dot(hot.astype(jnp.float32).astype(jnp.bfloat16), ref[...], NN)

    def only(condition, value):
        return jnp.where(condition, value, 0)

    side = QUART * (y // 2)
    quarter = pick(up_ref, 40, side, UNITS, 32, only(y % 2 == 0, QUART)) + pick(
        down_ref, 40, side, UNITS, 32, only(y % 2 == 1, QUART)
    )
    rows = pick(key_ref, 40, 0, 32, 0, only(core == 0, 32)) + pick(
        value_ref, 40, 0, 32, 0, only(core == 1, 32)
    )
    unit_ref[...] = (rows + quarter).astype(jnp.bfloat16)
    whole_ref[...] = (
        pick(up_ref, 32, HALF, UNITS, 0, HALF) + pick(down_ref, 32, HALF, UNITS, 16, HALF)
    ).astype(jnp.bfloat16)


def units(spot, key_rows, value_rows, up_rows, down_rows):
    vmem = pl.BlockSpec(memory_space=pltpu.VMEM)
    return pl.pallas_call(
        units_kernel,
        out_shape=(
            jax.ShapeDtypeStruct((40, E), jnp.bfloat16),
            jax.ShapeDtypeStruct((32, E), jnp.bfloat16),
        ),
        in_specs=[pl.BlockSpec(memory_space=pltpu.SMEM)] + [vmem] * 4,
        out_specs=(vmem, vmem),
        compiler_params=pltpu.CompilerParams(vmem_limit_bytes=56 * 1024 * 1024),
        name="pick_units",
    )(spot, key_rows, value_rows, up_rows, down_rows)


def gelu(x):
    return 0.5 * x * (1.0 + jnp.tanh(0.7978845608028654 * (x + 0.044715 * (x * x * x))))


def place_kernel(meta, recv_ref, gain_ref, raw_ref, normed_ref):
    first = PER_DEV * meta[32]
    for n in range(NY * NC * PER_DEV):
        slot = meta[n] - first

        @pl.when((slot >= 0) & (slot < PER_DEV))
        def _():
            raw_ref[slot] = recv_ref[n // PER_DEV]

    floats = raw_ref[...].astype(jnp.float32)
    mean = jnp.mean(floats * floats, axis=-1, keepdims=True)
    normed_ref[...] = (floats * lax.rsqrt(mean + EPS) * gain_ref[...]).astype(jnp.bfloat16)


def place(meta, recv, gain):
    vmem = pl.BlockSpec(memory_space=pltpu.VMEM)
    rows = jax.ShapeDtypeStruct((PER_DEV, NLEN, E), jnp.bfloat16)
    return pl.pallas_call(
        place_kernel,
        out_shape=(rows, rows),
        in_specs=[pl.BlockSpec(memory_space=pltpu.SMEM), vmem, vmem],
        out_specs=(vmem, vmem),
        compiler_params=pltpu.CompilerParams(vmem_limit_bytes=8 * 1024 * 1024),
        name="place_rows",
    )(meta, recv, gain)


def both_cores(mine, other):
    return jnp.concatenate([mine[...].reshape(ROWS, E), other[...].reshape(ROWS, E)])


def blocks_y(pairs):
    return [(up[...].reshape(256, E), down[...].reshape(256, E)) for up, down in pairs]


def blocks_x(pieces):
    out = []
    for one, two in zip(pieces[::2], pieces[1::2]):
        ups, downs = [], []
        for piece in (one, two):
            ups.append(piece[:, 0:16].reshape(128, E))
            downs.append(piece[:, 16:32].reshape(128, E))
        out.append((jnp.concatenate(ups), jnp.concatenate(downs)))
    return out


def multiply(normed, blocks):
    total = None
    for up, down in blocks:
        hidden = gelu(dot(normed, up, NT)).astype(jnp.bfloat16)
        part = dot(hidden, down, NN)
        total = part if total is None else total + part
    return total


def by_case(meta, even, odd, x_pieces, write):
    core, parity = meta[33], meta[34] % 2

    @pl.when((core == 0) & (parity == 0))
    def _():
        write(blocks_y(even))

    @pl.when((core == 0) & (parity == 1))
    def _():
        write(blocks_y(odd))

    @pl.when(core != 0)
    def _():
        write(blocks_x(x_pieces))


def early_kernel(meta, mine, other, own_a, own_b, left_a, left_b, right_a, right_b, acc_ref):
    normed = both_cores(mine, other)

    def write(blocks):
        acc_ref[...] = multiply(normed, blocks)

    by_case(
        meta,
        ((own_a, right_a), (own_b, right_b)),
        ((left_a, own_a), (left_b, own_b)),
        (own_a, own_b, left_a, left_b, right_a, right_b),
        write,
    )


def late_kernel(
    meta, raw, mine, other, acc, left_a, left_b, right_a, right_b, far_a, far_b, mine_ref, other_ref
):
    normed = both_cores(mine, other)

    def write(blocks):
        total = acc[...] + multiply(normed, blocks)
        mine_ref[...] = total[:ROWS] + raw[...].reshape(ROWS, E).astype(jnp.float32)
        other_ref[...] = total[ROWS:]

    by_case(
        meta,
        ((far_a, left_a), (far_b, left_b)),
        ((right_a, far_a), (right_b, far_b)),
        (far_a, far_b),
        write,
    )


def encode_part(kernel, outs, meta, *arrays):
    vmem = pl.BlockSpec(memory_space=pltpu.VMEM)
    return pl.pallas_call(
        kernel,
        out_shape=outs,
        in_specs=[pl.BlockSpec(memory_space=pltpu.SMEM)] + [vmem] * len(arrays),
        out_specs=jax.tree.map(lambda _: vmem, outs),
        compiler_params=pltpu.CompilerParams(vmem_limit_bytes=14 * 1024 * 1024),
        name=kernel.__name__,
    )(meta, *arrays)


GROUP = 4
CHUNK = 4
CUT = 2 * GROUP
LAST = 256
LIMIT = 48 * 1024 * 1024


def attend_kernel(
    mine_ref, other_ref, w_hbm, q_hbm, g_hbm, att_hbm, gq_hbm, ge_ref, w, q_ref, g_ref, kv, gkv, att, gq, sems, outs
):
    def fetch(i):
        return pltpu.make_async_copy(
            w_hbm.at[i * CUT : (i + 1) * CUT], w.at[i * CUT : (i + 1) * CUT], sems.at[i]
        )

    loads = [fetch(i) for i in range(2 * HEADS // CUT)]
    loads.append(pltpu.make_async_copy(q_hbm, q_ref, sems.at[len(loads)]))
    loads.append(pltpu.make_async_copy(g_hbm, g_ref, sems.at[len(loads)]))
    for copy in loads:
        copy.start()

    enc = (mine_ref[...] + other_ref[...]).astype(jnp.bfloat16)
    first = lax.broadcasted_iota(jnp.int32, (NPC * NLEN, CH_DEV * CL), 1) < CL
    half = NPC * NLEN

    def fold(full):
        return jnp.where(first, full[:half], full[half:])

    def spread(part):
        zero = jnp.zeros_like(part)
        return jnp.concatenate([jnp.where(first, part, zero), jnp.where(first, zero, part)])

    for base in range(0, HEADS, GROUP):
        loads[base // GROUP].wait()
        for j in range(2 * base, 2 * (base + GROUP), CHUNK):
            rows = w[j : j + CHUNK].reshape(CHUNK * HD, E)
            kv[:, j * HD : (j + CHUNK) * HD] = dot(enc, rows, NT).astype(jnp.bfloat16)
        if base == 0:
            loads[-2].wait()
            loads[-1].wait()
        heads = range(base, base + GROUP)
        cols = [slice(h * HD, (h + 1) * HD) for h in heads]
        kcols = [slice(2 * h * HD, (2 * h + 1) * HD) for h in heads]
        vcols = [slice((2 * h + 1) * HD, (2 * h + 2) * HD) for h in heads]
        scores = [fold(dot(kv[:, k], q_ref[:, c], NT)) * SCALE for c, k in zip(cols, kcols)]
        grad_probs = [fold(dot(kv[:, v], g_ref[:, c], NT)) for c, v in zip(cols, vcols)]
        exponent = [jnp.exp(s - jnp.max(s, axis=0, keepdims=True)) for s in scores]
        probs = [e * (1.0 / jnp.sum(e, axis=0, keepdims=True)) for e in exponent]
        delta = [jnp.sum(p * gp, axis=0, keepdims=True) for p, gp in zip(probs, grad_probs)]
        low = [spread(p).astype(jnp.bfloat16) for p in probs]
        grad_scores = [
            spread(p * (gp - d) * SCALE).astype(jnp.bfloat16)
            for p, gp, d in zip(probs, grad_probs, delta)
        ]
        for i, (c, k, v) in enumerate(zip(cols, kcols, vcols)):
            att[:, c] = dot(low[i], kv[:, v], TN).astype(jnp.bfloat16)
            gkv[:, v] = dot(low[i], g_ref[:, c], NN).astype(jnp.bfloat16)
            gq[:, c] = dot(grad_scores[i], kv[:, k], TN).astype(jnp.bfloat16)
            gkv[:, k] = dot(grad_scores[i], q_ref[:, c], NN).astype(jnp.bfloat16)
    stores = [
        pltpu.make_async_copy(att, att_hbm, outs.at[0]),
        pltpu.make_async_copy(gq, gq_hbm, outs.at[1]),
    ]
    for copy in stores:
        copy.start()
    rows = w[...].reshape(2 * HEADS * HD, E)
    for j in range(0, E, LAST):
        wide = slice(j, min(j + LAST, E))
        ge_ref[:, wide] = dot(gkv[...], rows[:, wide], NN).astype(jnp.bfloat16)
    for copy in stores:
        copy.wait()


def attend(mine, other, weights, queries, grads):
    tokens = CH_DEV * CL
    hbm = pl.BlockSpec(memory_space=pltpu.HBM)
    vmem = pl.BlockSpec(memory_space=pltpu.VMEM)
    wide = jax.ShapeDtypeStruct((tokens, HEADS * HD), jnp.bfloat16)
    full = pltpu.VMEM((tokens, HEADS * HD), jnp.bfloat16)
    both = pltpu.VMEM((ROWS, 2 * HEADS * HD), jnp.bfloat16)
    return pl.pallas_call(
        attend_kernel,
        out_shape=(wide, wide, jax.ShapeDtypeStruct((ROWS, E), jnp.bfloat16)),
        in_specs=[vmem, vmem, hbm, hbm, hbm],
        out_specs=(hbm, hbm, vmem),
        scratch_shapes=[
            pltpu.VMEM((2 * HEADS, HD, E), jnp.bfloat16),
            full,
            full,
            both,
            both,
            full,
            full,
            pltpu.SemaphoreType.DMA((2 * HEADS // CUT + 2,)),
            pltpu.SemaphoreType.DMA((2,)),
        ],
        compiler_params=pltpu.CompilerParams(vmem_limit_bytes=LIMIT),
        name="attend_spans",
    )(mine, other, weights, queries, grads)


def body(queries, neighbours, slots, gain, up, down, key_proj, value_proj, grads):
    z, x, y, c = (lax.axis_index(name) for name in ALL)
    group = NY * NC * PER_DEV
    here = jnp.stack([y * NC + c, c, y, x]).astype(jnp.int32)
    meta = jnp.concatenate([slots - (z * NX + x) * group, here])

    spot = (y * NC + c).astype(jnp.int32).reshape(1)
    unit, whole = units(spot, key_proj.T, value_proj.T, up.T, down)
    along_x = lax.all_gather(unit, "x", axis=0, tiled=False)
    kv_head = along_x[:, :32].reshape(HD, E)
    weights = lax.all_gather(kv_head, ("z", "c"), axis=0, tiled=False)

    ff_unit = jnp.where(c == 0, along_x[:, 32:].reshape(32, E), whole)
    own = lax.all_gather(ff_unit, "z", axis=0, tiled=False)
    own, rows = lax.optimization_barrier((own, neighbours))
    outgoing = send_blocks(meta, rows.reshape(PER_DEV, NLEN, E))
    own_a, own_b = own[: NZ // 2], own[NZ // 2 :]
    left_a, right_b = ring(own_a, 1), ring(own_b, -1)
    left_b, right_a = ring(own_b, 1), ring(own_a, -1)
    left_a, right_b, outgoing = lax.optimization_barrier((left_a, right_b, outgoing))
    recv = lax.all_to_all(outgoing, ("y", "c"), 0, 0, tiled=True)
    raw, normed = place(meta, recv, gain.reshape(1, E))
    other = swap(normed)
    far_a, far_b = ring(left_a, 1), ring(right_b, -1)
    near = (left_a, left_b, right_a, right_b)
    one = jax.ShapeDtypeStruct((ROWS, E), jnp.float32)
    two = jax.ShapeDtypeStruct((2 * ROWS, E), jnp.float32)
    acc = encode_part(early_kernel, two, meta, normed, other, own_a, own_b, *near)
    mine, given = encode_part(
        late_kernel, (one, one), meta, raw, normed, other, acc, *near, far_a, far_b
    )
    return attend(mine, swap(given), weights, queries, grads)


def solution(mesh):
    wide = Mesh(mesh.devices.reshape(NZ, NX, NY, NC), ALL)
    rows = P(ALL, None)
    fsdp = ("z", "x")
    in_specs = (
        rows,
        rows,
        P(fsdp),
        P(),
        P(None, fsdp),
        P(fsdp, None),
        P(None, fsdp),
        P(None, fsdp),
        rows,
    )
    return jax.shard_map(
        body, mesh=wide, in_specs=in_specs, out_specs=(rows, rows, rows), check_vma=False
    )
```

```python
import jax
import jax.numpy as jnp
from jax import lax
from jax.experimental import pallas as pl
from jax.experimental.pallas import tpu as pltpu
from jax.sharding import Mesh, PartitionSpec as P

E = 896
HEADS = 16
HD = 128
CL = 64
NLEN = 64
NPC = 2
CH_DEV = 2
NZ, NX, NY, NC = 16, 4, 4, 2
PER_DEV = CH_DEV * NPC
ROWS = PER_DEV * NLEN
UNITS = 28
HALF = UNITS // 2
QUART = UNITS // 4
EPS = 1e-06
SCALE = HD ** (-0.5)
ALL = ("z", "x", "y", "c")
NT = (((1,), (1,)), ((), ()))
NN = (((1,), (0,)), ((), ()))
TN = (((0,), (0,)), ((), ()))


def dot(a, b, dims):
    return lax.dot_general(a, b, dims, preferred_element_type=jnp.float32)


def ring_pairs(step):
    pairs = []
    for x in range(NX):
        for y in range(NY):
            pairs.append(((x * NY + y) * NC, (x * NY + (y + step) % NY) * NC))
            pairs.append(((x * NY + y) * NC + 1, ((x + step) % NX * NY + y) * NC + 1))
    return pairs


def ring(rows, step):
    return lax.ppermute(rows, ("x", "y", "c"), ring_pairs(step))


def swap(rows):
    return lax.ppermute(rows, "c", [(0, 1), (1, 0)])


def send_kernel(meta, raw_ref, out_ref):
    for i in range(PER_DEV):
        out_ref[meta[PER_DEV * meta[32] + i] // PER_DEV] = raw_ref[i]


def send_blocks(meta, raw):
    vmem = pl.BlockSpec(memory_space=pltpu.VMEM)
    return pl.pallas_call(
        send_kernel,
        out_shape=jax.ShapeDtypeStruct((NY * NC, NLEN, E), jnp.bfloat16),
        in_specs=[pl.BlockSpec(memory_space=pltpu.SMEM), vmem],
        out_specs=vmem,
        compiler_params=pltpu.CompilerParams(vmem_limit_bytes=8 * 1024 * 1024),
        name="send_blocks",
    )(meta, raw)


def units_kernel(spot, key_ref, value_ref, up_ref, down_ref, unit_ref, whole_ref):
    core, y = spot[0] % 2, spot[0] // 2 % NY

    def pick(ref, count, start, rows, offset, length):
        to = lax.broadcasted_iota(jnp.int32, (count, rows), 0) - offset
        source = lax.broadcasted_iota(jnp.int32, (count, rows), 1) - start
        hot = (to == source) & (to >= 0) & (to < length)
        return dot(hot.astype(jnp.float32).astype(jnp.bfloat16), ref[...], NN)

    def only(condition, value):
        return jnp.where(condition, value, 0)

    side = QUART * (y // 2)
    quarter = pick(up_ref, 40, side, UNITS, 32, only(y % 2 == 0, QUART)) + pick(
        down_ref, 40, side, UNITS, 32, only(y % 2 == 1, QUART)
    )
    rows = pick(key_ref, 40, 0, 32, 0, only(core == 0, 32)) + pick(
        value_ref, 40, 0, 32, 0, only(core == 1, 32)
    )
    unit_ref[...] = (rows + quarter).astype(jnp.bfloat16)
    whole_ref[...] = (
        pick(up_ref, 32, HALF, UNITS, 0, HALF) + pick(down_ref, 32, HALF, UNITS, 16, HALF)
    ).astype(jnp.bfloat16)


def units(spot, key_rows, value_rows, up_rows, down_rows):
    vmem = pl.BlockSpec(memory_space=pltpu.VMEM)
    return pl.pallas_call(
        units_kernel,
        out_shape=(
            jax.ShapeDtypeStruct((40, E), jnp.bfloat16),
            jax.ShapeDtypeStruct((32, E), jnp.bfloat16),
        ),
        in_specs=[pl.BlockSpec(memory_space=pltpu.SMEM)] + [vmem] * 4,
        out_specs=(vmem, vmem),
        compiler_params=pltpu.CompilerParams(vmem_limit_bytes=56 * 1024 * 1024),
        name="pick_units",
    )(spot, key_rows, value_rows, up_rows, down_rows)


def gelu(x):
    return 0.5 * x * (1.0 + jnp.tanh(0.7978845608028654 * (x + 0.044715 * (x * x * x))))


def place_kernel(meta, recv_ref, gain_ref, raw_ref, normed_ref):
    first = PER_DEV * meta[32]
    for n in range(NY * NC * PER_DEV):
        slot = meta[n] - first

        @pl.when((slot >= 0) & (slot < PER_DEV))
        def _():
            raw_ref[slot] = recv_ref[n // PER_DEV]

    floats = raw_ref[...].astype(jnp.float32)
    mean = jnp.mean(floats * floats, axis=-1, keepdims=True)
    normed_ref[...] = (floats * lax.rsqrt(mean + EPS) * gain_ref[...]).astype(jnp.bfloat16)


def place(meta, recv, gain):
    vmem = pl.BlockSpec(memory_space=pltpu.VMEM)
    rows = jax.ShapeDtypeStruct((PER_DEV, NLEN, E), jnp.bfloat16)
    return pl.pallas_call(
        place_kernel,
        out_shape=(rows, rows),
        in_specs=[pl.BlockSpec(memory_space=pltpu.SMEM), vmem, vmem],
        out_specs=(vmem, vmem),
        compiler_params=pltpu.CompilerParams(vmem_limit_bytes=8 * 1024 * 1024),
        name="place_rows",
    )(meta, recv, gain)


def both_cores(mine, other):
    return jnp.concatenate([mine[...].reshape(ROWS, E), other[...].reshape(ROWS, E)])


def blocks_y(pairs):
    return [(up[...].reshape(256, E), down[...].reshape(256, E)) for up, down in pairs]


def blocks_x(pieces):
    out = []
    for one, two in zip(pieces[::2], pieces[1::2]):
        ups, downs = [], []
        for piece in (one, two):
            ups.append(piece[:, 0:16].reshape(128, E))
            downs.append(piece[:, 16:32].reshape(128, E))
        out.append((jnp.concatenate(ups), jnp.concatenate(downs)))
    return out


def multiply(normed, blocks):
    total = None
    for up, down in blocks:
        hidden = gelu(dot(normed, up, NT)).astype(jnp.bfloat16)
        part = dot(hidden, down, NN)
        total = part if total is None else total + part
    return total


def by_case(meta, even, odd, x_pieces, write):
    core, parity = meta[33], meta[34] % 2

    @pl.when((core == 0) & (parity == 0))
    def _():
        write(blocks_y(even))

    @pl.when((core == 0) & (parity == 1))
    def _():
        write(blocks_y(odd))

    @pl.when(core != 0)
    def _():
        write(blocks_x(x_pieces))


def early_kernel(meta, mine, other, own_a, own_b, left_a, left_b, right_a, right_b, acc_ref):
    normed = both_cores(mine, other)

    def write(blocks):
        acc_ref[...] = multiply(normed, blocks)

    by_case(
        meta,
        ((own_a, right_a), (own_b, right_b)),
        ((left_a, own_a), (left_b, own_b)),
        (own_a, own_b, left_a, left_b, right_a, right_b),
        write,
    )


def late_kernel(
    meta, raw, mine, other, acc, left_a, left_b, right_a, right_b, far_a, far_b, mine_ref, other_ref
):
    normed = both_cores(mine, other)

    def write(blocks):
        total = acc[...] + multiply(normed, blocks)
        mine_ref[...] = total[:ROWS] + raw[...].reshape(ROWS, E).astype(jnp.float32)
        other_ref[...] = total[ROWS:]

    by_case(
        meta,
        ((far_a, left_a), (far_b, left_b)),
        ((right_a, far_a), (right_b, far_b)),
        (far_a, far_b),
        write,
    )


def encode_part(kernel, outs, meta, *arrays):
    vmem = pl.BlockSpec(memory_space=pltpu.VMEM)
    return pl.pallas_call(
        kernel,
        out_shape=outs,
        in_specs=[pl.BlockSpec(memory_space=pltpu.SMEM)] + [vmem] * len(arrays),
        out_specs=jax.tree.map(lambda _: vmem, outs),
        compiler_params=pltpu.CompilerParams(vmem_limit_bytes=14 * 1024 * 1024),
        name=kernel.__name__,
    )(meta, *arrays)


GROUP = 4
CHUNK = 4
CUT = 2 * GROUP
LAST = 256
LIMIT = 48 * 1024 * 1024


def attend_kernel(
    mine_ref, other_ref, w_hbm, q_hbm, g_hbm, att_hbm, gq_hbm, ge_ref, w, q_ref, g_ref, kv, gkv, att, gq, sems, outs
):
    def fetch(i):
        return pltpu.make_async_copy(
            w_hbm.at[i * CUT : (i + 1) * CUT], w.at[i * CUT : (i + 1) * CUT], sems.at[i]
        )

    loads = [fetch(i) for i in range(2 * HEADS // CUT)]
    loads.append(pltpu.make_async_copy(q_hbm, q_ref, sems.at[len(loads)]))
    loads.append(pltpu.make_async_copy(g_hbm, g_ref, sems.at[len(loads)]))
    for copy in loads:
        copy.start()

    enc = (mine_ref[...] + other_ref[...]).astype(jnp.bfloat16)
    first = lax.broadcasted_iota(jnp.int32, (NPC * NLEN, CH_DEV * CL), 1) < CL
    half = NPC * NLEN

    def fold(full):
        return jnp.where(first, full[:half], full[half:])

    def spread(part):
        zero = jnp.zeros_like(part)
        return jnp.concatenate([jnp.where(first, part, zero), jnp.where(first, zero, part)])

    for base in range(0, HEADS, GROUP):
        loads[base // GROUP].wait()
        for j in range(2 * base, 2 * (base + GROUP), CHUNK):
            rows = w[j : j + CHUNK].reshape(CHUNK * HD, E)
            kv[:, j * HD : (j + CHUNK) * HD] = dot(enc, rows, NT).astype(jnp.bfloat16)
        if base == 0:
            loads[-2].wait()
            loads[-1].wait()
        heads = range(base, base + GROUP)
        cols = [slice(h * HD, (h + 1) * HD) for h in heads]
        kcols = [slice(2 * h * HD, (2 * h + 1) * HD) for h in heads]
        vcols = [slice((2 * h + 1) * HD, (2 * h + 2) * HD) for h in heads]
        scores = [fold(dot(kv[:, k], q_ref[:, c], NT)) * SCALE for c, k in zip(cols, kcols)]
        grad_probs = [fold(dot(kv[:, v], g_ref[:, c], NT)) for c, v in zip(cols, vcols)]
        exponent = [jnp.exp(s - jnp.max(s, axis=0, keepdims=True)) for s in scores]
        probs = [e * (1.0 / jnp.sum(e, axis=0, keepdims=True)) for e in exponent]
        delta = [jnp.sum(p * gp, axis=0, keepdims=True) for p, gp in zip(probs, grad_probs)]
        low = [spread(p).astype(jnp.bfloat16) for p in probs]
        grad_scores = [
            spread(p * (gp - d) * SCALE).astype(jnp.bfloat16)
            for p, gp, d in zip(probs, grad_probs, delta)
        ]
        for i, (c, k, v) in enumerate(zip(cols, kcols, vcols)):
            att[:, c] = dot(low[i], kv[:, v], TN).astype(jnp.bfloat16)
            gkv[:, v] = dot(low[i], g_ref[:, c], NN).astype(jnp.bfloat16)
            gq[:, c] = dot(grad_scores[i], kv[:, k], TN).astype(jnp.bfloat16)
            gkv[:, k] = dot(grad_scores[i], q_ref[:, c], NN).astype(jnp.bfloat16)
    stores = [
        pltpu.make_async_copy(att, att_hbm, outs.at[0]),
        pltpu.make_async_copy(gq, gq_hbm, outs.at[1]),
    ]
    for copy in stores:
        copy.start()
    rows = w[...].reshape(2 * HEADS * HD, E)
    for j in range(0, E, LAST):
        wide = slice(j, min(j + LAST, E))
        ge_ref[:, wide] = dot(gkv[...], rows[:, wide], NN).astype(jnp.bfloat16)
    for copy in stores:
        copy.wait()


def attend(mine, other, weights, queries, grads):
    tokens = CH_DEV * CL
    hbm = pl.BlockSpec(memory_space=pltpu.HBM)
    vmem = pl.BlockSpec(memory_space=pltpu.VMEM)
    wide = jax.ShapeDtypeStruct((tokens, HEADS * HD), jnp.bfloat16)
    full = pltpu.VMEM((tokens, HEADS * HD), jnp.bfloat16)
    both = pltpu.VMEM((ROWS, 2 * HEADS * HD), jnp.bfloat16)
    return pl.pallas_call(
        attend_kernel,
        out_shape=(wide, wide, jax.ShapeDtypeStruct((ROWS, E), jnp.bfloat16)),
        in_specs=[vmem, vmem, hbm, hbm, hbm],
        out_specs=(hbm, hbm, vmem),
        scratch_shapes=[
            pltpu.VMEM((2 * HEADS, HD, E), jnp.bfloat16),
            full,
            full,
            both,
            both,
            full,
            full,
            pltpu.SemaphoreType.DMA((2 * HEADS // CUT + 2,)),
            pltpu.SemaphoreType.DMA((2,)),
        ],
        compiler_params=pltpu.CompilerParams(vmem_limit_bytes=LIMIT),
        name="attend_spans",
    )(mine, other, weights, queries, grads)


def body(queries, neighbours, slots, gain, up, down, key_proj, value_proj, grads):
    z, x, y, c = (lax.axis_index(name) for name in ALL)
    group = NY * NC * PER_DEV
    here = jnp.stack([y * NC + c, c, y, x]).astype(jnp.int32)
    meta = jnp.concatenate([slots - (z * NX + x) * group, here])

    spot = (y * NC + c).astype(jnp.int32).reshape(1)
    unit, whole = units(spot, key_proj.T, value_proj.T, up.T, down)
    along_x = lax.all_gather(unit, "x", axis=0, tiled=False)
    kv_head = along_x[:, :32].reshape(HD, E)
    weights = lax.all_gather(kv_head, ("z", "c"), axis=0, tiled=False)

    outgoing = send_blocks(meta, neighbours.reshape(PER_DEV, NLEN, E))
    ff_unit = jnp.where(c == 0, along_x[:, 32:].reshape(32, E), whole)
    ff_unit, outgoing = lax.optimization_barrier((ff_unit, outgoing))
    recv = lax.all_to_all(outgoing, ("y", "c"), 0, 0, tiled=True)
    own = lax.all_gather(ff_unit, "z", axis=0, tiled=False)
    own, recv = lax.optimization_barrier((own, recv))
    own_a, own_b = own[: NZ // 2], own[NZ // 2 :]
    left_a, right_b = ring(own_a, 1), ring(own_b, -1)
    left_b, right_a = ring(own_b, 1), ring(own_a, -1)
    left_a, right_b, recv = lax.optimization_barrier((left_a, right_b, recv))
    raw, normed = place(meta, recv, gain.reshape(1, E))
    other = swap(normed)
    far_a, far_b = ring(left_a, 1), ring(right_b, -1)
    near = (left_a, left_b, right_a, right_b)
    one = jax.ShapeDtypeStruct((ROWS, E), jnp.float32)
    two = jax.ShapeDtypeStruct((2 * ROWS, E), jnp.float32)
    acc = encode_part(early_kernel, two, meta, normed, other, own_a, own_b, *near)
    mine, given = encode_part(
        late_kernel, (one, one), meta, raw, normed, other, acc, *near, far_a, far_b
    )
    return attend(mine, swap(given), weights, queries, grads)


def solution(mesh):
    wide = Mesh(mesh.devices.reshape(NZ, NX, NY, NC), ALL)
    rows = P(ALL, None)
    fsdp = ("z", "x")
    in_specs = (
        rows,
        rows,
        P(fsdp),
        P(),
        P(None, fsdp),
        P(fsdp, None),
        P(None, fsdp),
        P(None, fsdp),
        rows,
    )
    return jax.shard_map(
        body, mesh=wide, in_specs=in_specs, out_specs=(rows, rows, rows), check_vma=False
    )
```

```python
import jax
import jax.numpy as jnp
from jax import lax
from jax.experimental import pallas as pl
from jax.experimental.pallas import tpu as pltpu
from jax.sharding import Mesh, PartitionSpec as P

E = 896
HEADS = 16
HD = 128
CL = 64
NLEN = 64
NPC = 2
CH_DEV = 2
NZ, NX, NY, NC = 16, 4, 4, 2
PER_DEV = CH_DEV * NPC
ROWS = PER_DEV * NLEN
GROUP_SLOTS = NY * NC * PER_DEV
UNITS = 28
HALF = UNITS // 2
QUART = UNITS // 4
EPS = 1e-06
SCALE = HD ** (-0.5)
ALL = ("z", "x", "y", "c")
NT = (((1,), (1,)), ((), ()))
NN = (((1,), (0,)), ((), ()))
TN = (((0,), (0,)), ((), ()))


def dot(a, b, dims):
    return lax.dot_general(a, b, dims, preferred_element_type=jnp.float32)


def ring_pairs(step):
    pairs = []
    for x in range(NX):
        for y in range(NY):
            pairs.append(((x * NY + y) * NC, (x * NY + (y + step) % NY) * NC))
            pairs.append(((x * NY + y) * NC + 1, ((x + step) % NX * NY + y) * NC + 1))
    return pairs


def ring(rows, step):
    return lax.ppermute(rows, ("x", "y", "c"), ring_pairs(step))


def swap(rows):
    return lax.ppermute(rows, "c", [(0, 1), (1, 0)])


def units_kernel(
    slots, spot, raw_ref, key_ref, value_ref, up_ref, down_ref, unit_ref, whole_ref, out_ref
):
    for i in range(PER_DEV):
        out_ref[slots[PER_DEV * spot[0] + i] % GROUP_SLOTS // PER_DEV] = raw_ref[i]
    core, y = spot[0] % 2, spot[0] // 2 % NY

    def pick(ref, count, start, rows, offset, length):
        to = lax.broadcasted_iota(jnp.int32, (count, rows), 0) - offset
        source = lax.broadcasted_iota(jnp.int32, (count, rows), 1) - start
        hot = (to == source) & (to >= 0) & (to < length)
        return dot(hot.astype(jnp.float32).astype(jnp.bfloat16), ref[...], NN)

    def only(condition, value):
        return jnp.where(condition, value, 0)

    side = QUART * (y // 2)
    quarter = pick(up_ref, 40, side, UNITS, 32, only(y % 2 == 0, QUART)) + pick(
        down_ref, 40, side, UNITS, 32, only(y % 2 == 1, QUART)
    )
    rows = pick(key_ref, 40, 0, 32, 0, only(core == 0, 32)) + pick(
        value_ref, 40, 0, 32, 0, only(core == 1, 32)
    )
    unit_ref[...] = (rows + quarter).astype(jnp.bfloat16)
    whole_ref[...] = (
        pick(up_ref, 32, HALF, UNITS, 0, HALF) + pick(down_ref, 32, HALF, UNITS, 16, HALF)
    ).astype(jnp.bfloat16)


def units(slots, spot, raw, key_rows, value_rows, up_rows, down_rows):
    vmem = pl.BlockSpec(memory_space=pltpu.VMEM)
    return pl.pallas_call(
        units_kernel,
        out_shape=(
            jax.ShapeDtypeStruct((40, E), jnp.bfloat16),
            jax.ShapeDtypeStruct((32, E), jnp.bfloat16),
            jax.ShapeDtypeStruct((NY * NC, NLEN, E), jnp.bfloat16),
        ),
        in_specs=[pl.BlockSpec(memory_space=pltpu.SMEM)] * 2 + [vmem] * 5,
        out_specs=(vmem, vmem, vmem),
        compiler_params=pltpu.CompilerParams(vmem_limit_bytes=56 * 1024 * 1024),
        name="pick_units",
    )(slots, spot, raw, key_rows, value_rows, up_rows, down_rows)


def gelu(x):
    return 0.5 * x * (1.0 + jnp.tanh(0.7978845608028654 * (x + 0.044715 * (x * x * x))))


def place_kernel(slots, spot, recv_ref, gain_ref, raw_ref, normed_ref):
    first = PER_DEV * spot[0]
    for n in range(GROUP_SLOTS):
        slot = slots[n] % GROUP_SLOTS - first

        @pl.when((slot >= 0) & (slot < PER_DEV))
        def _():
            raw_ref[slot] = recv_ref[n // PER_DEV]

    floats = raw_ref[...].astype(jnp.float32)
    mean = jnp.mean(floats * floats, axis=-1, keepdims=True)
    normed_ref[...] = (floats * lax.rsqrt(mean + EPS) * gain_ref[...]).astype(jnp.bfloat16)


def place(slots, spot, recv, gain):
    vmem = pl.BlockSpec(memory_space=pltpu.VMEM)
    rows = jax.ShapeDtypeStruct((PER_DEV, NLEN, E), jnp.bfloat16)
    return pl.pallas_call(
        place_kernel,
        out_shape=(rows, rows),
        in_specs=[pl.BlockSpec(memory_space=pltpu.SMEM)] * 2 + [vmem, vmem],
        out_specs=(vmem, vmem),
        compiler_params=pltpu.CompilerParams(vmem_limit_bytes=8 * 1024 * 1024),
        name="place_rows",
    )(slots, spot, recv, gain)


def both_cores(mine, other):
    return jnp.concatenate([mine[...].reshape(ROWS, E), other[...].reshape(ROWS, E)])


def blocks_y(pairs):
    return [(up[...].reshape(256, E), down[...].reshape(256, E)) for up, down in pairs]


def blocks_x(pieces):
    out = []
    for one, two in zip(pieces[::2], pieces[1::2]):
        ups, downs = [], []
        for piece in (one, two):
            ups.append(piece[:, 0:16].reshape(128, E))
            downs.append(piece[:, 16:32].reshape(128, E))
        out.append((jnp.concatenate(ups), jnp.concatenate(downs)))
    return out


def multiply(normed, blocks):
    total = None
    for up, down in blocks:
        hidden = gelu(dot(normed, up, NT)).astype(jnp.bfloat16)
        part = dot(hidden, down, NN)
        total = part if total is None else total + part
    return total


def by_case(spot, even, odd, x_pieces, write):
    core, parity = spot[0] % 2, spot[0] // 2 % 2

    @pl.when((core == 0) & (parity == 0))
    def _():
        write(blocks_y(even))

    @pl.when((core == 0) & (parity == 1))
    def _():
        write(blocks_y(odd))

    @pl.when(core != 0)
    def _():
        write(blocks_x(x_pieces))


def early_kernel(spot, mine, other, own_a, own_b, left_a, left_b, right_a, right_b, acc_ref):
    normed = both_cores(mine, other)

    def write(blocks):
        acc_ref[...] = multiply(normed, blocks)

    by_case(
        spot,
        ((own_a, right_a), (own_b, right_b)),
        ((left_a, own_a), (left_b, own_b)),
        (own_a, own_b, left_a, left_b, right_a, right_b),
        write,
    )


def late_kernel(
    spot, raw, mine, other, acc, left_a, left_b, right_a, right_b, far_a, far_b, mine_ref, other_ref
):
    normed = both_cores(mine, other)

    def write(blocks):
        total = acc[...] + multiply(normed, blocks)
        mine_ref[...] = total[:ROWS] + raw[...].reshape(ROWS, E).astype(jnp.float32)
        other_ref[...] = total[ROWS:]

    by_case(
        spot,
        ((far_a, left_a), (far_b, left_b)),
        ((right_a, far_a), (right_b, far_b)),
        (far_a, far_b),
        write,
    )


def encode_part(kernel, outs, spot, *arrays):
    vmem = pl.BlockSpec(memory_space=pltpu.VMEM)
    return pl.pallas_call(
        kernel,
        out_shape=outs,
        in_specs=[pl.BlockSpec(memory_space=pltpu.SMEM)] + [vmem] * len(arrays),
        out_specs=jax.tree.map(lambda _: vmem, outs),
        compiler_params=pltpu.CompilerParams(vmem_limit_bytes=14 * 1024 * 1024),
        name=kernel.__name__,
    )(spot, *arrays)


GROUP = 4
CHUNK = 4
CUT = 2 * GROUP
LAST = 256
LIMIT = 48 * 1024 * 1024


def attend_kernel(
    mine_ref, other_ref, w_hbm, q_hbm, g_hbm, att_hbm, gq_hbm, ge_ref, w, q_ref, g_ref, kv, gkv, att, gq, sems, outs
):
    def fetch(i):
        return pltpu.make_async_copy(
            w_hbm.at[i * CUT : (i + 1) * CUT], w.at[i * CUT : (i + 1) * CUT], sems.at[i]
        )

    loads = [fetch(i) for i in range(2 * HEADS // CUT)]
    loads.append(pltpu.make_async_copy(q_hbm, q_ref, sems.at[len(loads)]))
    loads.append(pltpu.make_async_copy(g_hbm, g_ref, sems.at[len(loads)]))
    for copy in loads:
        copy.start()

    enc = (mine_ref[...] + other_ref[...]).astype(jnp.bfloat16)
    first = lax.broadcasted_iota(jnp.int32, (NPC * NLEN, CH_DEV * CL), 1) < CL
    half = NPC * NLEN

    def fold(full):
        return jnp.where(first, full[:half], full[half:])

    def spread(part):
        zero = jnp.zeros_like(part)
        return jnp.concatenate([jnp.where(first, part, zero), jnp.where(first, zero, part)])

    for base in range(0, HEADS, GROUP):
        loads[base // GROUP].wait()
        for j in range(2 * base, 2 * (base + GROUP), CHUNK):
            rows = w[j : j + CHUNK].reshape(CHUNK * HD, E)
            kv[:, j * HD : (j + CHUNK) * HD] = dot(enc, rows, NT).astype(jnp.bfloat16)
        if base == 0:
            loads[-2].wait()
            loads[-1].wait()
        heads = range(base, base + GROUP)
        cols = [slice(h * HD, (h + 1) * HD) for h in heads]
        kcols = [slice(2 * h * HD, (2 * h + 1) * HD) for h in heads]
        vcols = [slice((2 * h + 1) * HD, (2 * h + 2) * HD) for h in heads]
        scores = [fold(dot(kv[:, k], q_ref[:, c], NT)) * SCALE for c, k in zip(cols, kcols)]
        grad_probs = [fold(dot(kv[:, v], g_ref[:, c], NT)) for c, v in zip(cols, vcols)]
        exponent = [jnp.exp(s - jnp.max(s, axis=0, keepdims=True)) for s in scores]
        probs = [e * (1.0 / jnp.sum(e, axis=0, keepdims=True)) for e in exponent]
        delta = [jnp.sum(p * gp, axis=0, keepdims=True) for p, gp in zip(probs, grad_probs)]
        low = [spread(p).astype(jnp.bfloat16) for p in probs]
        grad_scores = [
            spread(p * (gp - d) * SCALE).astype(jnp.bfloat16)
            for p, gp, d in zip(probs, grad_probs, delta)
        ]
        for i, (c, k, v) in enumerate(zip(cols, kcols, vcols)):
            att[:, c] = dot(low[i], kv[:, v], TN).astype(jnp.bfloat16)
            gkv[:, v] = dot(low[i], g_ref[:, c], NN).astype(jnp.bfloat16)
            gq[:, c] = dot(grad_scores[i], kv[:, k], TN).astype(jnp.bfloat16)
            gkv[:, k] = dot(grad_scores[i], q_ref[:, c], NN).astype(jnp.bfloat16)
    stores = [
        pltpu.make_async_copy(att, att_hbm, outs.at[0]),
        pltpu.make_async_copy(gq, gq_hbm, outs.at[1]),
    ]
    for copy in stores:
        copy.start()
    rows = w[...].reshape(2 * HEADS * HD, E)
    for j in range(0, E, LAST):
        wide = slice(j, min(j + LAST, E))
        ge_ref[:, wide] = dot(gkv[...], rows[:, wide], NN).astype(jnp.bfloat16)
    for copy in stores:
        copy.wait()


def attend(mine, other, weights, queries, grads):
    tokens = CH_DEV * CL
    hbm = pl.BlockSpec(memory_space=pltpu.HBM)
    vmem = pl.BlockSpec(memory_space=pltpu.VMEM)
    wide = jax.ShapeDtypeStruct((tokens, HEADS * HD), jnp.bfloat16)
    full = pltpu.VMEM((tokens, HEADS * HD), jnp.bfloat16)
    both = pltpu.VMEM((ROWS, 2 * HEADS * HD), jnp.bfloat16)
    return pl.pallas_call(
        attend_kernel,
        out_shape=(wide, wide, jax.ShapeDtypeStruct((ROWS, E), jnp.bfloat16)),
        in_specs=[vmem, vmem, hbm, hbm, hbm],
        out_specs=(hbm, hbm, vmem),
        scratch_shapes=[
            pltpu.VMEM((2 * HEADS, HD, E), jnp.bfloat16),
            full,
            full,
            both,
            both,
            full,
            full,
            pltpu.SemaphoreType.DMA((2 * HEADS // CUT + 2,)),
            pltpu.SemaphoreType.DMA((2,)),
        ],
        compiler_params=pltpu.CompilerParams(vmem_limit_bytes=LIMIT),
        name="attend_spans",
    )(mine, other, weights, queries, grads)


def body(queries, neighbours, slots, gain, up, down, key_proj, value_proj, grads):
    y, c = lax.axis_index("y"), lax.axis_index("c")
    spot = (y * NC + c).astype(jnp.int32).reshape(1)
    rows = neighbours.reshape(PER_DEV, NLEN, E)
    unit, whole, outgoing = units(slots, spot, rows, key_proj.T, value_proj.T, up.T, down)
    along_x = lax.all_gather(unit, "x", axis=0, tiled=False)
    kv_head = along_x[:, :32].reshape(HD, E)
    weights = lax.all_gather(kv_head, ("z", "c"), axis=0, tiled=False)

    ff_unit = jnp.where(c == 0, along_x[:, 32:].reshape(32, E), whole)
    ff_unit, outgoing = lax.optimization_barrier((ff_unit, outgoing))
    recv = lax.all_to_all(outgoing, ("y", "c"), 0, 0, tiled=True)
    own = lax.all_gather(ff_unit, "z", axis=0, tiled=False)
    own, recv = lax.optimization_barrier((own, recv))
    own_a, own_b = own[: NZ // 2], own[NZ // 2 :]
    left_a, right_b = ring(own_a, 1), ring(own_b, -1)
    left_b, right_a = ring(own_b, 1), ring(own_a, -1)
    left_a, right_b, recv = lax.optimization_barrier((left_a, right_b, recv))
    raw, normed = place(slots, spot, recv, gain.reshape(1, E))
    other = swap(normed)
    far_a, far_b = ring(left_a, 1), ring(right_b, -1)
    near = (left_a, left_b, right_a, right_b)
    one = jax.ShapeDtypeStruct((ROWS, E), jnp.float32)
    two = jax.ShapeDtypeStruct((2 * ROWS, E), jnp.float32)
    acc = encode_part(early_kernel, two, spot, normed, other, own_a, own_b, *near)
    mine, given = encode_part(
        late_kernel, (one, one), spot, raw, normed, other, acc, *near, far_a, far_b
    )
    return attend(mine, swap(given), weights, queries, grads)


def solution(mesh):
    wide = Mesh(mesh.devices.reshape(NZ, NX, NY, NC), ALL)
    rows = P(ALL, None)
    fsdp = ("z", "x")
    in_specs = (
        rows,
        rows,
        P(fsdp),
        P(),
        P(None, fsdp),
        P(fsdp, None),
        P(None, fsdp),
        P(None, fsdp),
        rows,
    )
    return jax.shard_map(
        body, mesh=wide, in_specs=in_specs, out_specs=(rows, rows, rows), check_vma=False
    )
```

```python
import jax
import jax.numpy as jnp
from jax import lax
from jax.experimental import pallas as pl
from jax.experimental.pallas import tpu as pltpu
from jax.sharding import Mesh, PartitionSpec as P

E = 896
HEADS = 16
HD = 128
CL = 64
NLEN = 64
NPC = 2
CH_DEV = 2
NZ, NX, NY, NC = 16, 4, 4, 2
PER_DEV = CH_DEV * NPC
ROWS = PER_DEV * NLEN
GROUP_SLOTS = NY * NC * PER_DEV
UNITS = 28
HALF = UNITS // 2
QUART = UNITS // 4
EPS = 1e-06
SCALE = HD ** (-0.5)
ALL = ("z", "x", "y", "c")
NT = (((1,), (1,)), ((), ()))
NN = (((1,), (0,)), ((), ()))
TN = (((0,), (0,)), ((), ()))


def dot(a, b, dims):
    return lax.dot_general(a, b, dims, preferred_element_type=jnp.float32)


def ring_pairs(step):
    pairs = []
    for x in range(NX):
        for y in range(NY):
            pairs.append(((x * NY + y) * NC, (x * NY + (y + step) % NY) * NC))
            pairs.append(((x * NY + y) * NC + 1, ((x + step) % NX * NY + y) * NC + 1))
    return pairs


def ring(rows, step):
    return lax.ppermute(rows, ("x", "y", "c"), ring_pairs(step))


def swap(rows):
    return lax.ppermute(rows, "c", [(0, 1), (1, 0)])


def units_kernel(
    slots, spot, raw_ref, key_ref, value_ref, up_ref, down_ref, unit_ref, whole_ref, out_ref
):
    for i in range(PER_DEV):
        out_ref[slots[PER_DEV * spot[0] + i] % GROUP_SLOTS // PER_DEV] = raw_ref[i]
    core, y = spot[0] % 2, spot[0] // 2 % NY

    def pick(ref, count, start, rows, offset, length):
        to = lax.broadcasted_iota(jnp.int32, (count, rows), 0) - offset
        source = lax.broadcasted_iota(jnp.int32, (count, rows), 1) - start
        hot = (to == source) & (to >= 0) & (to < length)
        return dot(hot.astype(jnp.float32).astype(jnp.bfloat16), ref[...], NN)

    def only(condition, value):
        return jnp.where(condition, value, 0)

    side = QUART * (y // 2)
    quarter = pick(up_ref, 40, side, UNITS, 32, only(y % 2 == 0, QUART)) + pick(
        down_ref, 40, side, UNITS, 32, only(y % 2 == 1, QUART)
    )
    rows = pick(key_ref, 40, 0, 32, 0, only(core == 0, 32)) + pick(
        value_ref, 40, 0, 32, 0, only(core == 1, 32)
    )
    unit_ref[...] = (rows + quarter).astype(jnp.bfloat16)
    whole_ref[...] = (
        pick(up_ref, 32, HALF, UNITS, 0, HALF) + pick(down_ref, 32, HALF, UNITS, 16, HALF)
    ).astype(jnp.bfloat16)


def units(slots, spot, raw, key_rows, value_rows, up_rows, down_rows):
    vmem = pl.BlockSpec(memory_space=pltpu.VMEM)
    return pl.pallas_call(
        units_kernel,
        out_shape=(
            jax.ShapeDtypeStruct((40, E), jnp.bfloat16),
            jax.ShapeDtypeStruct((32, E), jnp.bfloat16),
            jax.ShapeDtypeStruct((NY * NC, NLEN, E), jnp.bfloat16),
        ),
        in_specs=[pl.BlockSpec(memory_space=pltpu.SMEM)] * 2 + [vmem] * 5,
        out_specs=(vmem, vmem, vmem),
        compiler_params=pltpu.CompilerParams(vmem_limit_bytes=56 * 1024 * 1024),
        name="pick_units",
    )(slots, spot, raw, key_rows, value_rows, up_rows, down_rows)


def gelu(x):
    return 0.5 * x * (1.0 + jnp.tanh(0.7978845608028654 * (x + 0.044715 * (x * x * x))))


def place_kernel(slots, spot, recv_ref, gain_ref, raw_ref, normed_ref):
    first = PER_DEV * spot[0]
    for n in range(GROUP_SLOTS):
        slot = slots[n] % GROUP_SLOTS - first

        @pl.when((slot >= 0) & (slot < PER_DEV))
        def _():
            raw_ref[slot] = recv_ref[n // PER_DEV]

    floats = raw_ref[...].astype(jnp.float32)
    mean = jnp.mean(floats * floats, axis=-1, keepdims=True)
    normed_ref[...] = (floats * lax.rsqrt(mean + EPS) * gain_ref[...]).astype(jnp.bfloat16)


def place(slots, spot, recv, gain):
    vmem = pl.BlockSpec(memory_space=pltpu.VMEM)
    rows = jax.ShapeDtypeStruct((PER_DEV, NLEN, E), jnp.bfloat16)
    return pl.pallas_call(
        place_kernel,
        out_shape=(rows, rows),
        in_specs=[pl.BlockSpec(memory_space=pltpu.SMEM)] * 2 + [vmem, vmem],
        out_specs=(vmem, vmem),
        compiler_params=pltpu.CompilerParams(vmem_limit_bytes=8 * 1024 * 1024),
        name="place_rows",
    )(slots, spot, recv, gain)


def both_cores(mine, other):
    return jnp.concatenate([mine[...].reshape(ROWS, E), other[...].reshape(ROWS, E)])


def blocks_y(pairs):
    return [(up[...].reshape(256, E), down[...].reshape(256, E)) for up, down in pairs]


def blocks_x(pieces):
    out = []
    for one, two in zip(pieces[::2], pieces[1::2]):
        ups, downs = [], []
        for piece in (one, two):
            ups.append(piece[:, 0:16].reshape(128, E))
            downs.append(piece[:, 16:32].reshape(128, E))
        out.append((jnp.concatenate(ups), jnp.concatenate(downs)))
    return out


def multiply(normed, blocks):
    total = None
    for up, down in blocks:
        hidden = gelu(dot(normed, up, NT)).astype(jnp.bfloat16)
        part = dot(hidden, down, NN)
        total = part if total is None else total + part
    return total


def by_case(spot, even, odd, x_pieces, write):
    core, parity = spot[0] % 2, spot[0] // 2 % 2

    @pl.when((core == 0) & (parity == 0))
    def _():
        write(blocks_y(even))

    @pl.when((core == 0) & (parity == 1))
    def _():
        write(blocks_y(odd))

    @pl.when(core != 0)
    def _():
        write(blocks_x(x_pieces))


def early_kernel(spot, mine, other, own_a, own_b, left_a, left_b, right_a, right_b, acc_ref):
    normed = both_cores(mine, other)

    def write(blocks):
        acc_ref[...] = multiply(normed, blocks)

    by_case(
        spot,
        ((own_a, right_a), (own_b, right_b)),
        ((left_a, own_a), (left_b, own_b)),
        (own_a, own_b, left_a, left_b, right_a, right_b),
        write,
    )


def late_kernel(
    spot, raw, mine, other, acc, left_a, left_b, right_a, right_b, far_a, far_b, mine_ref, other_ref
):
    normed = both_cores(mine, other)

    def write(blocks):
        total = acc[...] + multiply(normed, blocks)
        mine_ref[...] = total[:ROWS] + raw[...].reshape(ROWS, E).astype(jnp.float32)
        other_ref[...] = total[ROWS:]

    by_case(
        spot,
        ((far_a, left_a), (far_b, left_b)),
        ((right_a, far_a), (right_b, far_b)),
        (far_a, far_b),
        write,
    )


def encode_part(kernel, outs, spot, *arrays):
    vmem = pl.BlockSpec(memory_space=pltpu.VMEM)
    return pl.pallas_call(
        kernel,
        out_shape=outs,
        in_specs=[pl.BlockSpec(memory_space=pltpu.SMEM)] + [vmem] * len(arrays),
        out_specs=jax.tree.map(lambda _: vmem, outs),
        compiler_params=pltpu.CompilerParams(vmem_limit_bytes=14 * 1024 * 1024),
        name=kernel.__name__,
    )(spot, *arrays)


GROUP = 4
CHUNK = 4
CUT = 2 * GROUP
LAST = 256
LIMIT = 48 * 1024 * 1024


def attend_kernel(
    mine_ref, other_ref, w_hbm, q_hbm, g_hbm, att_hbm, gq_hbm, ge_ref, w, q_ref, g_ref, kv, gkv, att, gq, sems, outs
):
    def fetch(i):
        return pltpu.make_async_copy(
            w_hbm.at[i * CUT : (i + 1) * CUT], w.at[i * CUT : (i + 1) * CUT], sems.at[i]
        )

    loads = [fetch(i) for i in range(2 * HEADS // CUT)]
    loads.append(pltpu.make_async_copy(q_hbm, q_ref, sems.at[len(loads)]))
    loads.append(pltpu.make_async_copy(g_hbm, g_ref, sems.at[len(loads)]))
    for copy in loads:
        copy.start()

    enc = (mine_ref[...] + other_ref[...]).astype(jnp.bfloat16)
    first = lax.broadcasted_iota(jnp.int32, (NPC * NLEN, CH_DEV * CL), 1) < CL
    half = NPC * NLEN

    def fold(full):
        return jnp.where(first, full[:half], full[half:])

    def spread(part):
        zero = jnp.zeros_like(part)
        return jnp.concatenate([jnp.where(first, part, zero), jnp.where(first, zero, part)])

    for base in range(0, HEADS, GROUP):
        loads[base // GROUP].wait()
        for j in range(2 * base, 2 * (base + GROUP), CHUNK):
            rows = w[j : j + CHUNK].reshape(CHUNK * HD, E)
            kv[:, j * HD : (j + CHUNK) * HD] = dot(enc, rows, NT).astype(jnp.bfloat16)
        if base == 0:
            loads[-2].wait()
            loads[-1].wait()
        heads = range(base, base + GROUP)
        cols = [slice(h * HD, (h + 1) * HD) for h in heads]
        kcols = [slice(2 * h * HD, (2 * h + 1) * HD) for h in heads]
        vcols = [slice((2 * h + 1) * HD, (2 * h + 2) * HD) for h in heads]
        scores = [fold(dot(kv[:, k], q_ref[:, c], NT)) * SCALE for c, k in zip(cols, kcols)]
        grad_probs = [fold(dot(kv[:, v], g_ref[:, c], NT)) for c, v in zip(cols, vcols)]
        exponent = [jnp.exp(s - jnp.max(s, axis=0, keepdims=True)) for s in scores]
        probs = [e * (1.0 / jnp.sum(e, axis=0, keepdims=True)) for e in exponent]
        delta = [jnp.sum(p * gp, axis=0, keepdims=True) for p, gp in zip(probs, grad_probs)]
        low = [spread(p).astype(jnp.bfloat16) for p in probs]
        grad_scores = [
            spread(p * (gp - d) * SCALE).astype(jnp.bfloat16)
            for p, gp, d in zip(probs, grad_probs, delta)
        ]
        for i, (c, k, v) in enumerate(zip(cols, kcols, vcols)):
            att[:, c] = dot(low[i], kv[:, v], TN).astype(jnp.bfloat16)
            gkv[:, v] = dot(low[i], g_ref[:, c], NN).astype(jnp.bfloat16)
            gq[:, c] = dot(grad_scores[i], kv[:, k], TN).astype(jnp.bfloat16)
            gkv[:, k] = dot(grad_scores[i], q_ref[:, c], NN).astype(jnp.bfloat16)
    stores = [
        pltpu.make_async_copy(att, att_hbm, outs.at[0]),
        pltpu.make_async_copy(gq, gq_hbm, outs.at[1]),
    ]
    for copy in stores:
        copy.start()
    rows = w[...].reshape(2 * HEADS * HD, E)
    for j in range(0, E, LAST):
        wide = slice(j, min(j + LAST, E))
        ge_ref[:, wide] = dot(gkv[...], rows[:, wide], NN).astype(jnp.bfloat16)
    for copy in stores:
        copy.wait()


def attend(mine, other, weights, queries, grads):
    tokens = CH_DEV * CL
    hbm = pl.BlockSpec(memory_space=pltpu.HBM)
    vmem = pl.BlockSpec(memory_space=pltpu.VMEM)
    wide = jax.ShapeDtypeStruct((tokens, HEADS * HD), jnp.bfloat16)
    full = pltpu.VMEM((tokens, HEADS * HD), jnp.bfloat16)
    both = pltpu.VMEM((ROWS, 2 * HEADS * HD), jnp.bfloat16)
    return pl.pallas_call(
        attend_kernel,
        out_shape=(wide, wide, jax.ShapeDtypeStruct((ROWS, E), jnp.bfloat16)),
        in_specs=[vmem, vmem, hbm, hbm, hbm],
        out_specs=(hbm, hbm, vmem),
        scratch_shapes=[
            pltpu.VMEM((2 * HEADS, HD, E), jnp.bfloat16),
            full,
            full,
            both,
            both,
            full,
            full,
            pltpu.SemaphoreType.DMA((2 * HEADS // CUT + 2,)),
            pltpu.SemaphoreType.DMA((2,)),
        ],
        compiler_params=pltpu.CompilerParams(vmem_limit_bytes=LIMIT),
        name="attend_spans",
    )(mine, other, weights, queries, grads)


def body(queries, neighbours, slots, gain, up, down, key_proj, value_proj, grads):
    y, c = lax.axis_index("y"), lax.axis_index("c")
    spot = (y * NC + c).astype(jnp.int32).reshape(1)
    rows = neighbours.reshape(PER_DEV, NLEN, E)
    unit, whole, outgoing = units(slots, spot, rows, key_proj.T, value_proj.T, up.T, down)
    recv = lax.all_to_all(outgoing, ("y", "c"), 0, 0, tiled=True)
    along_x = lax.all_gather(unit, "x", axis=0, tiled=False)
    along_x, recv = lax.optimization_barrier((along_x, recv))
    kv_head = along_x[:, :32].reshape(HD, E)
    weights = lax.all_gather(kv_head, ("z", "c"), axis=0, tiled=False)

    ff_unit = jnp.where(c == 0, along_x[:, 32:].reshape(32, E), whole)
    own = lax.all_gather(ff_unit, "z", axis=0, tiled=False)
    own_a, own_b = own[: NZ // 2], own[NZ // 2 :]
    left_a, right_b = ring(own_a, 1), ring(own_b, -1)
    left_b, right_a = ring(own_b, 1), ring(own_a, -1)
    left_a, right_b, recv = lax.optimization_barrier((left_a, right_b, recv))
    raw, normed = place(slots, spot, recv, gain.reshape(1, E))
    other = swap(normed)
    far_a, far_b = ring(left_a, 1), ring(right_b, -1)
    near = (left_a, left_b, right_a, right_b)
    one = jax.ShapeDtypeStruct((ROWS, E), jnp.float32)
    two = jax.ShapeDtypeStruct((2 * ROWS, E), jnp.float32)
    acc = encode_part(early_kernel, two, spot, normed, other, own_a, own_b, *near)
    mine, given = encode_part(
        late_kernel, (one, one), spot, raw, normed, other, acc, *near, far_a, far_b
    )
    return attend(mine, swap(given), weights, queries, grads)


def solution(mesh):
    wide = Mesh(mesh.devices.reshape(NZ, NX, NY, NC), ALL)
    rows = P(ALL, None)
    fsdp = ("z", "x")
    in_specs = (
        rows,
        rows,
        P(fsdp),
        P(),
        P(None, fsdp),
        P(fsdp, None),
        P(None, fsdp),
        P(None, fsdp),
        rows,
    )
    return jax.shard_map(
        body, mesh=wide, in_specs=in_specs, out_specs=(rows, rows, rows), check_vma=False
    )
```
